512 devices in a mesh: dp: 32 (over z_hi, x, y), seq: 16 (over z_lo, core).
Axes of the slice: x: 4, y: 4, z: 16 (z_hi: 2, z_lo: 8; z = z_hi * 8 + z_lo), core: 2. Of those that a mesh axis runs over, the one named last changes fastest.
Arguments:
- tokens: bfloat16 [32, 4096, 1280], P('dp', 'seq'), may hold values from -6 to 6
- out_grad: bfloat16 [32, 4096, 1280], P('dp', 'seq'), may hold values from -6 to 6
- logits: float32 [32, 16, 4096], P('dp', None, 'seq'), may hold values from -40 to 300
- router: bfloat16 [16, 1280], replicated, may hold values from -0.15625 to 0.15625
- w_in: bfloat16 [16, 1280, 5120], P('seq', None, 'dp'), may hold values from -0.15625 to 0.15625
- w_out: bfloat16 [16, 5120, 1280], P('seq', 'dp'), may hold values from -0.078125 to 0.078125
Outputs:
- token_grad: bfloat16 [32, 4096, 1280], P('dp', 'seq')
- router_grad: float32 [16, 1280], replicated
- w_in_grad: bfloat16 [16, 1280, 5120], P('seq', None, 'dp')
- w_out_grad: bfloat16 [16, 5120, 1280], P('seq', 'dp')
The draws below stay inside these ranges and needn't reach their ends.
All inputs are finite; a program needn't handle non-finite values.
Results may differ from the reference program's by a relative error of at most 0.022.
Values may be sent and summed in bfloat16 or wider, within the bound.
A program may use at most 64 MiB of HBM per device.

```python
import math
import jax
import jax.numpy as jnp
from jax import lax

D = 1280
F = 5120
EXPERTS = 16
TOKENS = 4096
CLIPS = 32


def draw_logits(key, part):
    key = jax.random.fold_in(key, 11)
    keys = jax.random.split(key, 3)
    spread = jnp.exp(jax.random.uniform(keys[0], (CLIPS, EXPERTS, 1), minval=0.0, maxval=1.386))
    position = jnp.arange(TOKENS, dtype=jnp.float32) / TOKENS
    shift = jax.random.uniform(keys[1], (CLIPS, 1, TOKENS), minval=-1.5, maxval=1.5) + 2.0 * position
    noise = jnp.clip(jax.random.normal(keys[2], (CLIPS, EXPERTS, TOKENS)), -6.0, 6.0)
    return spread * noise + shift


def block_levels(key, dims, shards, low, top_value):
    factor_of, own = 1.0, jax.random.fold_in(key, 6)
    for axis_at, parts in shards:
        steps = jnp.exp(jax.random.uniform(jax.random.fold_in(own, axis_at), (parts,), jnp.float32, low / len(shards), top_value / len(shards)))
        factor_of = factor_of * jnp.repeat(steps, dims[axis_at] // parts).reshape([-1 if axis == axis_at else 1 for axis in range(len(dims))])
    return factor_of


def bell_draw(own_key, shape, scale, limit, cuts=(), kind=jnp.bfloat16):
    entries = jax.random.normal(own_key, shape, jnp.float32) * scale
    if len(cuts) > 0:
        entries = block_levels(own_key, shape, cuts, -0.22, 0.18) * entries
    return jnp.clip(entries, min=-limit, max=limit).astype(kind)


def setup_inputs(seed: int = 0) -> dict:
    streams_of = jax.random.split(jax.random.key(seed), 7)
    return {
        "tokens": bell_draw(streams_of[0], (CLIPS, TOKENS, D), 1.0, 6.0, ((0, 32), (1, 16))),
        "out_grad": bell_draw(streams_of[1], (CLIPS, TOKENS, D), 1.0, 6.0, ((0, 32), (1, 16))),
        "logits": draw_logits(jax.random.fold_in(streams_of[6], 71), 0),
        "router": bell_draw(streams_of[3], (EXPERTS, D), D ** -0.5, 0.15625),
        "w_in": bell_draw(streams_of[4], (EXPERTS, D, F), D ** -0.5, 0.15625, ((0, 16), (2, 32))),
        "w_out": bell_draw(streams_of[5], (EXPERTS, F, D), F ** -0.5, 0.078125, ((0, 16), (1, 32))),
    }


def column_weights(logit_rows):
    combine = jax.nn.softmax(logit_rows, axis=0)
    col_peak = lax.optimization_barrier(jnp.max(logit_rows, axis=1, keepdims=True))
    raised = jnp.exp(logit_rows - col_peak)
    dispatch = (raised / lax.optimization_barrier(jnp.sum(raised, axis=1, keepdims=True))).astype(jnp.bfloat16)
    return (combine, dispatch)

def contract_first(left, right):
    return lax.dot_general(left, right, (((0,), (0,)), ((), ())), preferred_element_type=jnp.float32)

def contract_last(left, right):
    return lax.dot_general(left, right, (((1,), (1,)), ((), ())), preferred_element_type=jnp.float32)

def slot_side(inputs):
    tokens_clip, grads_clip, logit_rows = inputs
    combine, dispatch = column_weights(logit_rows)
    slot_sum = jnp.dot(dispatch, tokens_clip, preferred_element_type=jnp.float32)
    slot_back = jnp.dot(combine.astype(jnp.bfloat16), grads_clip, preferred_element_type=jnp.float32)
    return (slot_sum, slot_back)

def reference(tokens, out_grad, logits, router, w_in, w_out):
    slot_sum, slot_back = lax.map(slot_side, (tokens, out_grad, logits))
    slot_in = slot_sum.astype(jnp.bfloat16)
    back_low = slot_back.astype(jnp.bfloat16)
    in_wide = slot_in.astype(jnp.float32)
    back_wide = back_low.astype(jnp.float32)
    first_wide = w_in.astype(jnp.float32)
    second_wide = w_out.astype(jnp.float32)
    hidden_pre = jnp.einsum('ced,edf->cef', in_wide, first_wide)
    activated_f, gelu_back = jax.vjp(jax.nn.gelu, hidden_pre)
    activated = activated_f.astype(jnp.bfloat16).astype(jnp.float32)
    slot_out = jnp.einsum('cef,efd->ced', activated, second_wide).astype(jnp.bfloat16)
    act_back = jnp.einsum('ced,efd->cef', back_wide, second_wide)
    hidden_back = gelu_back(act_back)[0].astype(jnp.bfloat16).astype(jnp.float32)
    w_out_grad = jnp.einsum('cef,ced->efd', activated, back_wide).astype(jnp.bfloat16)
    w_in_grad = jnp.einsum('ced,cef->edf', in_wide, hidden_back).astype(jnp.bfloat16)
    slot_in_back = jnp.einsum('cef,edf->ced', hidden_back, first_wide).astype(jnp.bfloat16)

    def token_side(inputs):
        tokens_clip, grads_clip, logit_rows, outs_clip, backs_clip = inputs
        combine, dispatch = column_weights(logit_rows)
        combine_back = contract_last(outs_clip, grads_clip)
        logit_back = combine * (combine_back - lax.optimization_barrier(jnp.sum(combine * combine_back, axis=0, keepdims=True)))
        dispatch_back = contract_last(backs_clip, tokens_clip)
        weights = dispatch.astype(jnp.float32)
        slot_total = lax.optimization_barrier(jnp.sum(weights * dispatch_back, axis=1, keepdims=True))
        logit_back = (logit_back + weights * (dispatch_back - slot_total)).astype(jnp.bfloat16)
        router_part = jnp.dot(logit_back, tokens_clip, preferred_element_type=jnp.float32)
        token_part = contract_first(dispatch, backs_clip) + contract_first(logit_back, router)
        return ((token_part * 64.0).astype(jnp.bfloat16), router_part)
    token_grad, router_parts = lax.map(token_side, (tokens, out_grad, logits, slot_out, slot_in_back))
    router_grad = lax.optimization_barrier(jnp.sum(router_parts, axis=0)) / math.sqrt(CLIPS)
    return (token_grad, router_grad, w_in_grad, w_out_grad)
```

```python
import functools
import math

import jax
import jax.numpy as jnp
from jax import lax
from jax.experimental import pallas as pl
from jax.experimental.pallas import tpu as pltpu
from jax.sharding import PartitionSpec as P

MESH = pl.DeviceIdType.MESH
F32 = jnp.float32
BF16 = jnp.bfloat16

D = 1280
CH = D // 128
REC = 24
ZN = 16
XYN = 16
Z_ORDER = (8, 7, 9, 6, 10, 5, 11, 4, 12, 3, 13, 2, 14, 1, 15)
XY_ORDER = (
    (2, 2), (2, 1), (2, 3), (1, 2), (3, 2), (1, 1), (1, 3), (3, 1), (3, 3), (2, 0), (0, 2), (1, 0), (3, 0), (0, 1), (0, 3),
)


def low(value):
    return value.astype(BF16).astype(F32)


def dot(left, right, dims):
    return lax.dot_general(left, right, (dims, ((), ())), preferred_element_type=F32)


def kernel(
    tokens_hbm, grads_hbm, logits_hbm, router_hbm, w_in_hbm, w_out_hbm,
    token_grad_hbm, router_grad_ref, w_in_grad_hbm, w_out_grad_hbm,
    tokens_v, grads_v, logits_v, router_v, w_in_v, w_out_v, token_grad_v, w_in_grad_v, w_out_grad_v,
    sa, ra, sz, rz, sb, rb, wide, sc, rc, sd, rd, se, sf, rf, sg, rg, sh, rh, ri,
    in_sem, out_sem, send_sem, recv_sem,
):
    dp, sq = lax.axis_index("dp"), lax.axis_index("seq")
    zhi, xy = dp // 16, lax.rem(dp, 16)
    zlo, core = sq // 2, lax.rem(sq, 2)
    z = zhi * 8 + zlo
    x, y = xy // 4, lax.rem(xy, 4)

    def device(z_to, xy_to, core_to):
        return (z_to // 8 * 16 + xy_to, lax.rem(z_to, 8) * 2 + core_to)

    z_peers = [lax.rem(z + k, ZN) for k in Z_ORDER]
    xy_peers = [lax.rem(x + dx, 4) * 4 + lax.rem(y + dy, 4) for dx, dy in XY_ORDER]
    sibling = device(z, xy, 1 - core)

    loads = []
    for i, (src, dst) in enumerate(
        (
            (logits_hbm, logits_v),
            (tokens_hbm, tokens_v),
            (grads_hbm, grads_v),
            (router_hbm, router_v),
            (w_in_hbm, w_in_v),
            (w_out_hbm, w_out_v),
        )
    ):
        copy = pltpu.make_async_copy(src, dst, in_sem.at[i])
        copy.start()
        loads.append(copy)

    barrier = pltpu.get_barrier_semaphore()
    for z_to in z_peers:
        pl.semaphore_signal(barrier, inc=1, device_id=device(z_to, xy, core), device_id_type=MESH)
    for xy_to in xy_peers:
        pl.semaphore_signal(barrier, inc=1, device_id=device(z, xy_to, core), device_id_type=MESH)
    pl.semaphore_signal(barrier, inc=1, device_id=sibling, device_id_type=MESH)

    def send(stage, src, dst, to):
        pltpu.make_async_remote_copy(
            src_ref=src,
            dst_ref=dst,
            send_sem=send_sem.at[stage],
            recv_sem=recv_sem.at[stage],
            device_id=to,
            device_id_type=MESH,
        ).start()

    def wait(sem, ref):
        pltpu.make_async_copy(ref, ref, sem).wait()

    row = lax.broadcasted_iota(jnp.int32, (REC, 128), 0)
    lane = lax.broadcasted_iota(jnp.int32, (REC, 128), 1)

    def chunk(value, j):
        return value[:, j * 128 : (j + 1) * 128]

    def core_major(rows):
        return jnp.concatenate([rows[2 * j + p : 2 * j + p + 1] for p in range(2) for j in range(8)], axis=0)

    loads[0].wait()
    logits = core_major(logits_v[0])
    raised_c = jnp.exp(logits - jnp.max(logits, axis=0, keepdims=True))
    combine = raised_c / jnp.sum(raised_c, axis=0, keepdims=True)
    peak = low(jnp.max(logits, axis=1, keepdims=True))
    raised = jnp.exp(logits - peak)
    total = jnp.sum(raised, axis=1, keepdims=True)
    loads[1].wait()
    gathered = dot(raised.astype(BF16), tokens_v[0], ((1,), (0,)))
    loads[2].wait()
    backs = dot(combine.astype(BF16), grads_v[0], ((1,), (0,)))
    for j in range(CH):
        sa[pl.ds(j, 16, stride=REC), :] = chunk(gathered, j)
        sa[pl.ds(CH + j, 16, stride=REC), :] = chunk(backs, j)
    sa[pl.ds(20, 16, stride=REC), :] = jnp.broadcast_to(peak, (16, 128))
    sa[pl.ds(21, 16, stride=REC), :] = jnp.broadcast_to(total, (16, 128))
    for i in (22, 23):
        sa[pl.ds(i, 16, stride=REC), :] = jnp.zeros((16, 128), F32)
    loads[3].wait()
    router = core_major(router_v[...].astype(F32))
    loads[4].wait()
    loads[5].wait()

    pl.semaphore_wait(barrier, 31)

    send(0, sa.at[pl.ds((1 - core) * 192, 192)], ra, sibling)
    wait(recv_sem.at[0], ra)
    own = sa[pl.ds(pl.multiple_of(core * 192, 192), 192), :].reshape(8, REC, 128)
    other = ra[...].reshape(8, REC, 128)
    scaled = (row < CH) | (row == 21)
    top = jnp.maximum(own[:, 20:21, :], other[:, 20:21, :])
    both = own * jnp.where(scaled, jnp.exp(own[:, 20:21, :] - top), 1.0) + other * jnp.where(
        scaled, jnp.exp(other[:, 20:21, :] - top), 1.0
    )
    count = both[:, 21:22, :]
    both = jnp.where(row == 20, top, jnp.where(row == 22, count - low(count), both))
    sz[...] = both.astype(BF16)
    rz[pl.ds(z, 1)] = sz[pl.ds(zlo, 1)]

    for z_to in z_peers:
        send(1, sz.at[lax.rem(z_to, 8)], rz.at[z], device(z_to, xy, core))
    wait(recv_sem.at[1], rz.at[pl.ds(0, ZN - 1)])
    slots, tops, totals = [], [], []
    for h in range(2):
        part = rz[pl.ds(8 * h, 8)].astype(F32)
        peaks = part[:, 20:21, :]
        top = jnp.max(peaks, axis=0)
        factor = jnp.exp(peaks - top)
        count = jnp.sum(factor * (part[:, 21:22, :] + part[:, 22:23, :]), axis=0)
        summed = jnp.sum(part * jnp.where(row < CH, factor, 1.0), axis=0)
        slots.append(jnp.where(row < CH, summed / count, summed))
        tops.append(top)
        totals.append(count)
        sb[pl.ds(REC * h, REC), :] = slots[h]
    packed = sb[...].astype(BF16)
    rb[pl.ds(xy, 1)] = packed[None]

    for xy_to in xy_peers:
        send(2, rb.at[xy], rb.at[xy], device(z, xy_to, core))
    wait(recv_sem.at[2], rb.at[pl.ds(0, XYN - 1)])
    wide[...] = rb[...].astype(F32).reshape(XYN * 48, 128)

    def clips(first):
        return jnp.concatenate(
            [
                jnp.concatenate(
                    [wide[pl.ds(h * REC + first + j, 16, stride=48), :].astype(BF16) for j in range(CH)],
                    axis=1,
                )
                for h in range(2)
            ],
            axis=0,
        )

    every_in, every_back = clips(0), clips(CH)
    pre = dot(every_in, w_in_v[0], ((1,), (0,)))
    act_back = dot(every_back, w_out_v[0], ((1,), (1,)))
    slope = math.sqrt(2.0 / math.pi)
    bent = jnp.tanh(slope * (pre + 0.044715 * (pre * pre * pre)))
    activated = (0.5 * pre * (1.0 + bent)).astype(BF16)
    gelu_slope = 0.5 * (1.0 + bent) + 0.5 * pre * ((1.0 + bent) * (1.0 - bent)) * (
        slope * (1.0 + 3.0 * 0.044715 * (pre * pre))
    )
    hidden_back = (gelu_slope * act_back).astype(BF16)
    in_part = dot(hidden_back, w_in_v[0], ((1,), (1,)))
    out_part = dot(activated, w_out_v[0], ((1,), (0,)))
    for h in range(2):
        for j in range(CH):
            wide[pl.ds(h * REC + j, 16, stride=48), :] = chunk(in_part, j)[16 * h : 16 * h + 16]
            wide[pl.ds(h * REC + CH + j, 16, stride=48), :] = chunk(out_part, j)[16 * h : 16 * h + 16]
    sc[...] = wide[...].reshape(XYN, 48, 128).astype(BF16)
    rc[pl.ds(xy, 1)] = sc[pl.ds(xy, 1)]

    for xy_to in xy_peers:
        send(3, sc.at[xy_to], rc.at[xy], device(z, xy_to, core))
    w_out_grad_v[0] = dot(activated, every_back, ((0,), (0,))).astype(BF16)
    w_in_grad_v[0] = dot(every_in, hidden_back, ((0,), (0,))).astype(BF16)
    stores = [
        pltpu.make_async_copy(w_in_grad_v, w_in_grad_hbm, out_sem.at[0]),
        pltpu.make_async_copy(w_out_grad_v, w_out_grad_hbm, out_sem.at[1]),
        pltpu.make_async_copy(token_grad_v, token_grad_hbm, out_sem.at[2]),
    ]
    stores[0].start()
    stores[1].start()
    wait(recv_sem.at[3], rc.at[pl.ds(0, XYN - 1)])
    halves = jnp.sum(rc[...].astype(F32), axis=0)
    for h in range(2):
        half = halves[REC * h : REC * h + REC]
        dotted = jnp.sum(jnp.where(row < CH, low(half) * slots[h], 0.0), keepdims=True)
        half = jnp.where(row == 20, tops[h], half)
        half = jnp.where(row == 21, totals[h], half)
        half = jnp.where(row == 22, totals[h] - low(totals[h]), half)
        half = jnp.where(row == 23, jnp.where(lane < 64, dotted, dotted - low(dotted)), half)
        sd[pl.ds(h, 1)] = half.astype(BF16)[None]
    rd[pl.ds(z, 1)] = sd[pl.ds(zhi, 1)]

    for z_to in z_peers:
        send(4, sd.at[z_to // 8], rd.at[z], device(z_to, xy, core))
    wait(recv_sem.at[4], rd.at[pl.ds(0, ZN - 1)])
    first, second = rd[pl.ds(0, 8)].astype(F32), rd[pl.ds(8, 8)].astype(F32)
    both = first + second
    dotted = both[:, 23:24, 0:1] + both[:, 23:24, 64:65]
    both = jnp.where(row == 20, first, both)
    both = jnp.where(row == 21, first[:, 21:22, :] + first[:, 22:23, :], both)
    both = jnp.where(row == 23, dotted, both)
    mine = pl.ds(pl.multiple_of(core * 192, 192), 192)
    se[mine, :] = both.reshape(192, 128)

    send(5, se.at[mine], se.at[mine], sibling)
    wait(recv_sem.at[5], ra)

    def slot_rows(first):
        return jnp.concatenate([se[pl.ds(first + j, 16, stride=REC), :] for j in range(CH)], axis=1).astype(BF16)

    in_back, slot_out = slot_rows(0), slot_rows(CH)
    col_peak = se[pl.ds(20, 16, stride=REC), :][:, 0:1]
    col_total = se[pl.ds(21, 16, stride=REC), :][:, 0:1]
    slot_total = se[pl.ds(23, 16, stride=REC), :][:, 0:1]
    dispatch = (jnp.exp(logits - col_peak) / col_total).astype(BF16)
    weights = dispatch.astype(F32)
    combine_back = dot(slot_out, grads_v[0], ((1,), (1,)))
    dispatch_back = dot(in_back, tokens_v[0], ((1,), (1,)))
    logit_comb = combine * (combine_back - jnp.sum(combine * combine_back, axis=0, keepdims=True))
    logit_back = (logit_comb + weights * (dispatch_back - slot_total)).astype(BF16)
    router_part = dot(logit_back, tokens_v[0], ((1,), (0,)))
    for j in range(CH):
        ri[pl.ds(j, 16, stride=16), :] = chunk(router_part, j)
    for j in range(CH, 16):
        ri[pl.ds(j, 16, stride=16), :] = jnp.zeros((16, 128), F32)
    sf[...] = ri[...].reshape(16, 16, 128).astype(BF16)
    rf[pl.ds(xy, 1)] = sf[pl.ds(xy, 1)]

    for xy_to in xy_peers:
        send(6, sf.at[xy_to], rf.at[xy], device(z, xy_to, core))
    left = jnp.concatenate([weights, logit_back.astype(F32)], axis=0).astype(BF16)
    right = jnp.concatenate([in_back.astype(F32), router], axis=0).astype(BF16)
    token_grad_v[0] = (dot(left, right, ((0,), (0,))) * 64.0).astype(BF16)
    stores[2].start()
    wait(recv_sem.at[6], rf.at[pl.ds(0, XYN - 1)])
    sg[...] = jnp.sum(rf[...].astype(F32), axis=0)

    send(7, sg, rg, sibling)
    wait(recv_sem.at[7], rg)
    sh[...] = (sg[...] + rg[...]).astype(BF16)
    rh[pl.ds(z, 1)] = sh[...][None]
    for z_to in z_peers:
        send(8, sh, rh.at[z], device(z_to, xy, core))
    wait(recv_sem.at[8], rh.at[pl.ds(0, ZN - 1)])
    mine = pl.ds(pl.multiple_of((lax.rem(xy, 8) * 2 + xy // 8) * 16, 16), 16)
    ri[mine, :] = jnp.sum(rh[...].astype(F32), axis=0) / math.sqrt(32.0)

    for xy_to in xy_peers:
        send(9, ri.at[mine], ri.at[mine], device(z, xy_to, core))
    wait(recv_sem.at[9], ri.at[pl.ds(0, 240)])
    for j in range(CH):
        router_grad_ref[:, j * 128 : (j + 1) * 128] = ri[pl.ds(j, 16, stride=16), :]

    wait(send_sem.at[0], ra)
    wait(send_sem.at[1], rz.at[pl.ds(0, ZN - 1)])
    wait(send_sem.at[2], rb.at[pl.ds(0, XYN - 1)])
    wait(send_sem.at[3], rc.at[pl.ds(0, XYN - 1)])
    wait(send_sem.at[4], rd.at[pl.ds(0, ZN - 1)])
    wait(send_sem.at[5], ra)
    wait(send_sem.at[6], rf.at[pl.ds(0, XYN - 1)])
    wait(send_sem.at[7], rg)
    wait(send_sem.at[8], rh.at[pl.ds(0, ZN - 1)])
    wait(send_sem.at[9], ri.at[pl.ds(0, 240)])
    for copy in stores:
        copy.wait()


def local(tokens, out_grad, logits, router, w_in, w_out):
    hbm = pl.BlockSpec(memory_space=pl.ANY)
    inputs = (tokens, out_grad, logits, router, w_in, w_out)
    return pl.pallas_call(
        kernel,
        name="moe_back",
        out_shape=(
            jax.ShapeDtypeStruct(tokens.shape, BF16),
            jax.ShapeDtypeStruct(router.shape, F32),
            jax.ShapeDtypeStruct(w_in.shape, BF16),
            jax.ShapeDtypeStruct(w_out.shape, BF16),
        ),
        in_specs=[hbm] * 6,
        out_specs=(hbm, pl.BlockSpec(memory_space=pltpu.VMEM), hbm, hbm),
        scratch_shapes=[pltpu.VMEM(a.shape, a.dtype) for a in inputs]
        + [
            pltpu.VMEM(tokens.shape, BF16),
            pltpu.VMEM(w_in.shape, BF16),
            pltpu.VMEM(w_out.shape, BF16),
            pltpu.VMEM((16 * REC, 128), F32),
            pltpu.VMEM((8 * REC, 128), F32),
            pltpu.VMEM((8, REC, 128), BF16),
            pltpu.VMEM((ZN, REC, 128), BF16),
            pltpu.VMEM((2 * REC, 128), F32),
            pltpu.VMEM((XYN, 48, 128), BF16),
            pltpu.VMEM((XYN * 48, 128), F32),
            pltpu.VMEM((XYN, 48, 128), BF16),
            pltpu.VMEM((XYN, 48, 128), BF16),
            pltpu.VMEM((2, REC, 128), BF16),
            pltpu.VMEM((ZN, REC, 128), BF16),
            pltpu.VMEM((16 * REC, 128), F32),
            pltpu.VMEM((16, 16, 128), BF16),
            pltpu.VMEM((XYN, 16, 128), BF16),
            pltpu.VMEM((16, 128), F32),
            pltpu.VMEM((16, 128), F32),
            pltpu.VMEM((16, 128), BF16),
            pltpu.VMEM((ZN, 16, 128), BF16),
            pltpu.VMEM((16 * 16, 128), F32),
            pltpu.SemaphoreType.DMA((6,)),
            pltpu.SemaphoreType.DMA((3,)),
            pltpu.SemaphoreType.DMA((10,)),
            pltpu.SemaphoreType.DMA((10,)),
        ],
        compiler_params=pltpu.CompilerParams(
            collective_id=0, has_side_effects=True, vmem_limit_bytes=48 * 1024 * 1024
        ),
    )(*inputs)


def solution(mesh):
    return jax.shard_map(
        local,
        mesh=mesh,
        in_specs=(
            P("dp", "seq", None),
            P("dp", "seq", None),
            P("dp", None, "seq"),
            P(),
            P("seq", None, "dp"),
            P("seq", "dp", None),
        ),
        out_specs=(P("dp", "seq", None), P(), P("seq", None, "dp"), P("seq", "dp", None)),
        check_vma=False,
    )
```

```python
import functools
import math

import jax
import jax.numpy as jnp
from jax import lax
from jax.experimental import pallas as pl
from jax.experimental.pallas import tpu as pltpu
from jax.sharding import PartitionSpec as P

MESH = pl.DeviceIdType.MESH
F32 = jnp.float32
BF16 = jnp.bfloat16

D = 1280
CH = D // 128
PAIR = 4 * CH
REC = 24
ZN = 16
XYN = 16
Z_ORDER = (8, 7, 9, 6, 10, 5, 11, 4, 12, 3, 13, 2, 14, 1, 15)
XY_ORDER = (
    (2, 2), (2, 1), (2, 3), (1, 2), (3, 2), (1, 1), (1, 3), (3, 1), (3, 3), (2, 0), (0, 2), (1, 0), (3, 0), (0, 1), (0, 3),
)


def low(value):
    return value.astype(BF16).astype(F32)


def dot(left, right, dims):
    return lax.dot_general(left, right, (dims, ((), ())), preferred_element_type=F32)


def kernel(
    tokens_hbm, grads_hbm, logits_hbm, router_hbm, w_in_hbm, w_out_hbm,
    token_grad_hbm, router_grad_hbm, w_in_grad_hbm, w_out_grad_hbm,
    tokens_v, grads_v, logits_v, router_v, w_in_v, w_out_v, token_grad_v, router_grad_ref, w_in_grad_v, w_out_grad_v,
    sa, ra, sz, rz, sb, rb, wide, sc, rc, halves, sd, rd, se, rows, sf, rf, sh, rh, ri,
    in_sem, out_sem, send_sem, recv_sem,
):
    dp, sq = lax.axis_index("dp"), lax.axis_index("seq")
    zhi, xy = dp // 16, lax.rem(dp, 16)
    zlo, core = sq // 2, lax.rem(sq, 2)
    z = zhi * 8 + zlo
    x, y = xy // 4, lax.rem(xy, 4)

    def device(z_to, xy_to, core_to):
        return (z_to // 8 * 16 + xy_to, lax.rem(z_to, 8) * 2 + core_to)

    z_peers = [lax.rem(z + k, ZN) for k in Z_ORDER]
    xy_peers = [lax.rem(x + dx, 4) * 4 + lax.rem(y + dy, 4) for dx, dy in XY_ORDER]
    sibling = device(z, xy, 1 - core)

    loads = []
    for i, (src, dst) in enumerate(
        (
            (logits_hbm, logits_v),
            (tokens_hbm, tokens_v),
            (grads_hbm, grads_v),
            (router_hbm, router_v),
            (w_in_hbm, w_in_v),
            (w_out_hbm, w_out_v),
        )
    ):
        copy = pltpu.make_async_copy(src, dst, in_sem.at[i])
        copy.start()
        loads.append(copy)

    barrier = pltpu.get_barrier_semaphore()
    for z_to in z_peers:
        pl.semaphore_signal(barrier, inc=1, device_id=device(z_to, xy, core), device_id_type=MESH)
    for xy_to in xy_peers:
        pl.semaphore_signal(barrier, inc=1, device_id=device(z, xy_to, core), device_id_type=MESH)
    for xy_to in xy_peers:
        pl.semaphore_signal(barrier, inc=1, device_id=device(z, xy_to, 1 - core), device_id_type=MESH)
    pl.semaphore_signal(barrier, inc=1, device_id=sibling, device_id_type=MESH)

    def send(stage, src, dst, to):
        pltpu.make_async_remote_copy(
            src_ref=src,
            dst_ref=dst,
            send_sem=send_sem.at[stage],
            recv_sem=recv_sem.at[stage],
            device_id=to,
            device_id_type=MESH,
        ).start()

    def wait(sem, ref):
        pltpu.make_async_copy(ref, ref, sem).wait()

    row = lax.broadcasted_iota(jnp.int32, (REC, 128), 0)
    lane = lax.broadcasted_iota(jnp.int32, (REC, 128), 1)

    def chunk(value, j):
        return value[:, j * 128 : (j + 1) * 128]

    def core_major(rows):
        return jnp.concatenate([rows[2 * j + p : 2 * j + p + 1] for p in range(2) for j in range(8)], axis=0)

    loads[0].wait()
    logits = core_major(logits_v[0])
    raised_c = jnp.exp(logits - jnp.max(logits, axis=0, keepdims=True))
    combine = raised_c / jnp.sum(raised_c, axis=0, keepdims=True)
    peak = low(jnp.max(logits, axis=1, keepdims=True))
    raised = jnp.exp(logits - peak)
    total = jnp.sum(raised, axis=1, keepdims=True)
    loads[1].wait()
    gathered = dot(raised.astype(BF16), tokens_v[0], ((1,), (0,)))
    loads[2].wait()
    backs = dot(combine.astype(BF16), grads_v[0], ((1,), (0,)))
    for j in range(CH):
        sa[pl.ds(j, 16, stride=REC), :] = chunk(gathered, j)
        sa[pl.ds(CH + j, 16, stride=REC), :] = chunk(backs, j)
    sa[pl.ds(20, 16, stride=REC), :] = jnp.broadcast_to(peak, (16, 128))
    sa[pl.ds(21, 16, stride=REC), :] = jnp.broadcast_to(total, (16, 128))
    for i in (22, 23):
        sa[pl.ds(i, 16, stride=REC), :] = jnp.zeros((16, 128), F32)
    halves[pl.ds(PAIR, 8), :] = jnp.zeros((8, 128), F32)
    loads[3].wait()
    router = core_major(router_v[...].astype(F32))
    loads[4].wait()
    loads[5].wait()

    pl.semaphore_wait(barrier, 46)

    send(0, sa.at[pl.ds((1 - core) * 192, 192)], ra, sibling)
    wait(recv_sem.at[0], ra)
    own = sa[pl.ds(pl.multiple_of(core * 192, 192), 192), :].reshape(8, REC, 128)
    other = ra[...].reshape(8, REC, 128)
    scaled = (row < CH) | (row == 21)
    top = jnp.maximum(own[:, 20:21, :], other[:, 20:21, :])
    both = own * jnp.where(scaled, jnp.exp(own[:, 20:21, :] - top), 1.0) + other * jnp.where(
        scaled, jnp.exp(other[:, 20:21, :] - top), 1.0
    )
    count = both[:, 21:22, :]
    both = jnp.where(row == 20, top, jnp.where(row == 22, count - low(count), both))
    sz[...] = both.astype(BF16)
    rz[pl.ds(z, 1)] = sz[pl.ds(zlo, 1)]

    for z_to in z_peers:
        send(1, sz.at[lax.rem(z_to, 8)], rz.at[z], device(z_to, xy, core))
    wait(recv_sem.at[1], rz.at[pl.ds(0, ZN - 1)])
    slots, tops, totals = [], [], []
    for h in range(2):
        part = rz[pl.ds(8 * h, 8)].astype(F32)
        peaks = part[:, 20:21, :]
        top = jnp.max(peaks, axis=0)
        factor = jnp.exp(peaks - top)
        count = jnp.sum(factor * (part[:, 21:22, :] + part[:, 22:23, :]), axis=0)
        summed = jnp.sum(part * jnp.where(row < CH, factor, 1.0), axis=0)
        slots.append(jnp.where(row < CH, summed / count, summed))
        tops.append(top)
        totals.append(count)
        sb[pl.ds(2 * CH * h, 2 * CH), :] = slots[h][: 2 * CH]
    packed = sb[...].astype(BF16)
    rb[pl.ds(xy, 1)] = packed[None]

    for xy_to in xy_peers:
        send(2, rb.at[xy], rb.at[xy], device(z, xy_to, core))
    wait(recv_sem.at[2], rb.at[pl.ds(0, XYN - 1)])
    wide[...] = rb[...].astype(F32).reshape(XYN * PAIR, 128)

    def clips(first):
        return jnp.concatenate(
            [
                jnp.concatenate(
                    [wide[pl.ds(h * 2 * CH + first + j, 16, stride=PAIR), :].astype(BF16) for j in range(CH)],
                    axis=1,
                )
                for h in range(2)
            ],
            axis=0,
        )

    every_in, every_back = clips(0), clips(CH)
    pre = dot(every_in, w_in_v[0], ((1,), (1,)))
    act_back = dot(every_back, w_out_v[0], ((1,), (1,)))
    slope = math.sqrt(2.0 / math.pi)
    bent = jnp.tanh(slope * (pre + 0.044715 * (pre * pre * pre)))
    activated = (0.5 * pre * (1.0 + bent)).astype(BF16)
    gelu_slope = 0.5 * (1.0 + bent) + 0.5 * pre * ((1.0 + bent) * (1.0 - bent)) * (
        slope * (1.0 + 3.0 * 0.044715 * (pre * pre))
    )
    hidden_back = (gelu_slope * act_back).astype(BF16)
    in_part = dot(hidden_back, w_in_v[0], ((1,), (0,)))
    out_part = dot(activated, w_out_v[0], ((1,), (0,)))
    for h in range(2):
        for j in range(CH):
            wide[pl.ds(h * 2 * CH + j, 16, stride=PAIR), :] = chunk(in_part, j)[16 * h : 16 * h + 16]
            wide[pl.ds(h * 2 * CH + CH + j, 16, stride=PAIR), :] = chunk(out_part, j)[16 * h : 16 * h + 16]
    sc[...] = wide[...].reshape(XYN, PAIR, 128).astype(BF16)
    rc[pl.ds(xy, 1)] = sc[pl.ds(xy, 1)]

    for xy_to in xy_peers:
        send(3, sc.at[xy_to], rc.at[xy], device(z, xy_to, core))
    w_out_grad_v[0] = dot(activated, every_back, ((0,), (0,))).astype(BF16)
    w_in_grad_v[0] = dot(hidden_back, every_in, ((0,), (0,))).astype(BF16)
    stores = [
        pltpu.make_async_copy(w_in_grad_v, w_in_grad_hbm, out_sem.at[0]),
        pltpu.make_async_copy(w_out_grad_v, w_out_grad_hbm, out_sem.at[1]),
        pltpu.make_async_copy(token_grad_v, token_grad_hbm, out_sem.at[2]),
        pltpu.make_async_copy(router_grad_ref, router_grad_hbm, out_sem.at[3]),
    ]
    stores[0].start()
    stores[1].start()
    wait(recv_sem.at[3], rc.at[pl.ds(0, XYN - 1)])
    halves[pl.ds(0, PAIR), :] = jnp.sum(rc[...].astype(F32), axis=0)
    for h in range(2):
        half = halves[pl.ds(2 * CH * h, REC), :]
        dotted = jnp.sum(jnp.where(row < CH, low(half) * slots[h], 0.0), keepdims=True)
        half = jnp.where(row == 20, tops[h], half)
        half = jnp.where(row == 21, totals[h], half)
        half = jnp.where(row == 22, totals[h] - low(totals[h]), half)
        half = jnp.where(row == 23, jnp.where(lane < 64, dotted, dotted - low(dotted)), half)
        sd[pl.ds(h, 1)] = half.astype(BF16)[None]
    rd[pl.ds(z, 1)] = sd[pl.ds(zhi, 1)]

    for z_to in z_peers:
        send(4, sd.at[z_to // 8], rd.at[z], device(z_to, xy, core))
    wait(recv_sem.at[4], rd.at[pl.ds(0, ZN - 1)])
    first, second = rd[pl.ds(0, 8)].astype(F32), rd[pl.ds(8, 8)].astype(F32)
    both = first + second
    dotted = both[:, 23:24, 0:1] + both[:, 23:24, 64:65]
    both = jnp.where(row == 20, first, both)
    both = jnp.where(row == 21, first[:, 21:22, :] + first[:, 22:23, :], both)
    both = jnp.where(row == 23, dotted, both)
    mine = pl.ds(pl.multiple_of(core * 192, 192), 192)
    se[mine, :] = both.reshape(192, 128)

    send(5, se.at[mine], se.at[mine], sibling)
    wait(recv_sem.at[5], ra)

    def slot_rows(first):
        return jnp.concatenate([se[pl.ds(first + j, 16, stride=REC), :] for j in range(CH)], axis=1).astype(BF16)

    in_back, slot_out = slot_rows(0), slot_rows(CH)
    col_peak = se[pl.ds(20, 16, stride=REC), :][:, 0:1]
    col_total = se[pl.ds(21, 16, stride=REC), :][:, 0:1]
    slot_total = se[pl.ds(23, 16, stride=REC), :][:, 0:1]
    dispatch = (jnp.exp(logits - col_peak) / col_total).astype(BF16)
    weights = dispatch.astype(F32)
    combine_back = dot(slot_out, grads_v[0], ((1,), (1,)))
    dispatch_back = dot(in_back, tokens_v[0], ((1,), (1,)))
    logit_comb = combine * (combine_back - jnp.sum(combine * combine_back, axis=0, keepdims=True))
    logit_back = (logit_comb + weights * (dispatch_back - slot_total)).astype(BF16)
    router_part = dot(logit_back, tokens_v[0], ((1,), (0,)))
    for j in range(CH):
        rows[pl.ds(j, 16, stride=16), :] = chunk(router_part, j)
    for j in range(CH, 16):
        rows[pl.ds(j, 16, stride=16), :] = jnp.zeros((16, 128), F32)
    sf[...] = rows[...].reshape(16, 16, 128).astype(BF16)
    rf[pl.ds(xy, 1)] = sf[pl.ds(xy, 1)]

    for xy_to in xy_peers:
        send(6, sf.at[xy_to], rf.at[xy], device(z, xy_to, core))
    left = jnp.concatenate([weights, logit_back.astype(F32)], axis=0).astype(BF16)
    right = jnp.concatenate([in_back.astype(F32), router], axis=0).astype(BF16)
    token_grad_v[0] = (dot(left, right, ((0,), (0,))) * 64.0).astype(BF16)
    stores[2].start()
    wait(recv_sem.at[6], rf.at[pl.ds(0, XYN - 1)])
    sh[...] = jnp.sum(rf[...].astype(F32), axis=0).astype(BF16)
    rh[pl.ds(z, 1)] = sh[...][None]

    for z_to in z_peers:
        send(7, sh, rh.at[z], device(z_to, xy, core))
    wait(recv_sem.at[7], rh.at[pl.ds(0, ZN - 1)])
    place = core * 16 + lax.rem(xy, 8) * 2 + xy // 8
    ri[pl.ds(place, 1)] = jnp.sum(rh[...].astype(F32), axis=0).astype(BF16)[None]

    for xy_to in xy_peers:
        send(8, ri.at[place], ri.at[place], device(z, xy_to, core))
        send(8, ri.at[place], ri.at[place], device(z, xy_to, 1 - core))
    send(8, ri.at[place], ri.at[place], sibling)
    wait(recv_sem.at[8], ri.at[pl.ds(0, 31)])
    rows[...] = ((ri[pl.ds(0, 16)].astype(F32) + ri[pl.ds(16, 16)].astype(F32)) / math.sqrt(32.0)).reshape(256, 128)
    for j in range(CH):
        router_grad_ref[:, j * 128 : (j + 1) * 128] = rows[pl.ds(j, 16, stride=16), :]
    stores[3].start()

    wait(send_sem.at[0], ra)
    wait(send_sem.at[1], rz.at[pl.ds(0, ZN - 1)])
    wait(send_sem.at[2], rb.at[pl.ds(0, XYN - 1)])
    wait(send_sem.at[3], rc.at[pl.ds(0, XYN - 1)])
    wait(send_sem.at[4], rd.at[pl.ds(0, ZN - 1)])
    wait(send_sem.at[5], ra)
    wait(send_sem.at[6], rf.at[pl.ds(0, XYN - 1)])
    wait(send_sem.at[7], rh.at[pl.ds(0, ZN - 1)])
    wait(send_sem.at[8], ri.at[pl.ds(0, 31)])
    for copy in stores:
        copy.wait()


def store_kernel(*refs):
    sources, targets, sems = refs[:4], refs[4:8], refs[8]
    copies = []
    for a, b in zip(sources, targets):
        if len(a.shape) == 2:
            parts = [(a, b)]
        else:
            cut = a.shape[1] // 2
            parts = [(a.at[:, pl.ds(i * cut, cut)], b.at[:, pl.ds(i * cut, cut)]) for i in range(2)]
        for part, to in parts:
            copies.append(pltpu.make_async_copy(part, to, sems.at[len(copies)]))
            copies[-1].start()
    for copy in copies:
        copy.wait()


def local(tokens, out_grad, logits, router, w_in, w_out):
    anywhere = pl.BlockSpec(memory_space=pl.ANY)
    hbm = pl.BlockSpec(memory_space=pltpu.HBM)
    w_in = jnp.swapaxes(w_in, 1, 2)
    inputs = tuple(
        pltpu.with_memory_space_constraint(a, pltpu.HBM) for a in (tokens, out_grad, logits, router, w_in, w_out)
    )
    results = (
        jax.ShapeDtypeStruct(tokens.shape, BF16),
        jax.ShapeDtypeStruct(router.shape, F32),
        jax.ShapeDtypeStruct(w_in.shape, BF16),
        jax.ShapeDtypeStruct(w_out.shape, BF16),
    )
    made = pl.pallas_call(
        kernel,
        name="moe_back",
        out_shape=tuple(pltpu.VMEM(a.shape, a.dtype) for a in results),
        in_specs=[hbm] * 6,
        out_specs=(anywhere,) * 4,
        scratch_shapes=[pltpu.VMEM(a.shape, a.dtype) for a in inputs]
        + [
            pltpu.VMEM(tokens.shape, BF16),
            pltpu.VMEM(router.shape, F32),
            pltpu.VMEM(w_in.shape, BF16),
            pltpu.VMEM(w_out.shape, BF16),
            pltpu.VMEM((16 * REC, 128), F32),
            pltpu.VMEM((8 * REC, 128), F32),
            pltpu.VMEM((8, REC, 128), BF16),
            pltpu.VMEM((ZN, REC, 128), BF16),
            pltpu.VMEM((PAIR, 128), F32),
            pltpu.VMEM((XYN, PAIR, 128), BF16),
            pltpu.VMEM((XYN * PAIR, 128), F32),
            pltpu.VMEM((XYN, PAIR, 128), BF16),
            pltpu.VMEM((XYN, PAIR, 128), BF16),
            pltpu.VMEM((48, 128), F32),
            pltpu.VMEM((2, REC, 128), BF16),
            pltpu.VMEM((ZN, REC, 128), BF16),
            pltpu.VMEM((16 * REC, 128), F32),
            pltpu.VMEM((16 * 16, 128), F32),
            pltpu.VMEM((16, 16, 128), BF16),
            pltpu.VMEM((XYN, 16, 128), BF16),
            pltpu.VMEM((16, 128), BF16),
            pltpu.VMEM((ZN, 16, 128), BF16),
            pltpu.VMEM((2 * 16, 16, 128), BF16),
            pltpu.SemaphoreType.DMA((6,)),
            pltpu.SemaphoreType.DMA((4,)),
            pltpu.SemaphoreType.DMA((9,)),
            pltpu.SemaphoreType.DMA((9,)),
        ],
        compiler_params=pltpu.CompilerParams(
            collective_id=0, has_side_effects=True, vmem_limit_bytes=32 * 1024 * 1024
        ),
    )(*inputs)
    token_grad, router_grad, w_in_grad, w_out_grad = pl.pallas_call(
        store_kernel,
        name="store",
        out_shape=results,
        in_specs=[anywhere] * 4,
        out_specs=(hbm,) * 4,
        scratch_shapes=[pltpu.SemaphoreType.DMA((7,))],
    )(*(pltpu.with_memory_space_constraint(a, pltpu.VMEM) for a in made))
    return (token_grad, router_grad, jnp.swapaxes(w_in_grad, 1, 2), w_out_grad)


def solution(mesh):
    return jax.shard_map(
        local,
        mesh=mesh,
        in_specs=(
            P("dp", "seq", None),
            P("dp", "seq", None),
            P("dp", None, "seq"),
            P(),
            P("seq", None, "dp"),
            P("seq", "dp", None),
        ),
        out_specs=(P("dp", "seq", None), P(), P("seq", None, "dp"), P("seq", "dp", None)),
        check_vma=False,
    )
```

```python
import functools
import math

import jax
import jax.numpy as jnp
from jax import lax
from jax.experimental import pallas as pl
from jax.experimental.pallas import tpu as pltpu
from jax.sharding import PartitionSpec as P

MESH = pl.DeviceIdType.MESH
F32 = jnp.float32
BF16 = jnp.bfloat16

D = 1280
CH = D // 128
PAIR = 4 * CH
REC = 24
ZN = 16
XYN = 16
Z_ORDER = (8, 7, 9, 6, 10, 5, 11, 4, 12, 3, 13, 2, 14, 1, 15)
XY_ORDER = (
    (2, 2), (2, 1), (2, 3), (1, 2), (3, 2), (1, 1), (1, 3), (3, 1), (3, 3), (2, 0), (0, 2), (1, 0), (3, 0), (0, 1), (0, 3),
)


def low(value):
    return value.astype(BF16).astype(F32)


def dot(left, right, dims):
    return lax.dot_general(left, right, (dims, ((), ())), preferred_element_type=F32)


def kernel(
    tokens_hbm, grads_hbm, logits_hbm, router_hbm, w_in_hbm, w_out_hbm,
    token_grad_hbm, router_grad_hbm, w_in_grad_hbm, w_out_grad_hbm,
    tokens_v, grads_v, logits_v, router_v, w_in_v, w_out_v, token_grad_v, router_grad_ref, w_in_grad_v, w_out_grad_v,
    sa, ra, sz, rz, sb, rb, wide, sc, rc, halves, sd, rd, se, rows, sf, rf, sh, rh, ri,
    in_sem, out_sem, send_sem, recv_sem, near_sem, far_sem,
):
    dp, sq = lax.axis_index("dp"), lax.axis_index("seq")
    zhi, xy = dp // 16, lax.rem(dp, 16)
    zlo, core = sq // 2, lax.rem(sq, 2)
    z = zhi * 8 + zlo
    x, y = xy // 4, lax.rem(xy, 4)

    def device(z_to, xy_to, core_to):
        return (z_to // 8 * 16 + xy_to, lax.rem(z_to, 8) * 2 + core_to)

    z_peers = [lax.rem(z + k, ZN) for k in Z_ORDER]
    xy_peers = [lax.rem(x + dx, 4) * 4 + lax.rem(y + dy, 4) for dx, dy in XY_ORDER]
    sibling = device(z, xy, 1 - core)

    barrier = pltpu.get_barrier_semaphore()

    @pl.when(core == 0)
    def _():
        pl.semaphore_signal(barrier, inc=1, device_id=sibling, device_id_type=MESH)

    for z_to in z_peers:
        pl.semaphore_signal(barrier, inc=1, device_id=device(z_to, xy, 0), device_id_type=MESH)
    for xy_to in xy_peers:
        pl.semaphore_signal(barrier, inc=1, device_id=device(z, xy_to, 0), device_id_type=MESH)

    loads = []
    for i, (src, dst) in enumerate(
        (
            (logits_hbm, logits_v),
            (tokens_hbm, tokens_v),
            (grads_hbm, grads_v),
            (router_hbm, router_v),
            (w_in_hbm, w_in_v),
            (w_out_hbm, w_out_v),
        )
    ):
        copy = pltpu.make_async_copy(src, dst, in_sem.at[i])
        copy.start()
        loads.append(copy)

    @pl.when(core == 1)
    def _():
        pl.semaphore_wait(barrier, 1)
        pl.semaphore_signal(near_sem, inc=1, device_id=sibling, device_id_type=MESH)

    def send(stage, src, dst, to):
        pltpu.make_async_remote_copy(
            src_ref=src,
            dst_ref=dst,
            send_sem=send_sem.at[stage],
            recv_sem=recv_sem.at[stage],
            device_id=to,
            device_id_type=MESH,
        ).start()

    def wait(sem, ref):
        pltpu.make_async_copy(ref, ref, sem).wait()

    row = lax.broadcasted_iota(jnp.int32, (REC, 128), 0)
    lane = lax.broadcasted_iota(jnp.int32, (REC, 128), 1)

    def chunk(value, j):
        return value[:, j * 128 : (j + 1) * 128]

    def core_major(rows):
        return jnp.concatenate([rows[2 * j + p : 2 * j + p + 1] for p in range(2) for j in range(8)], axis=0)

    loads[0].wait()
    logits = core_major(logits_v[0])
    raised_c = jnp.exp(logits - jnp.max(logits, axis=0, keepdims=True))
    combine = raised_c / jnp.sum(raised_c, axis=0, keepdims=True)
    peak = low(jnp.max(logits, axis=1, keepdims=True))
    raised = jnp.exp(logits - peak)
    total = jnp.sum(raised, axis=1, keepdims=True)
    loads[1].wait()
    gathered = dot(raised.astype(BF16), tokens_v[0], ((1,), (0,)))
    loads[2].wait()
    backs = dot(combine.astype(BF16), grads_v[0], ((1,), (0,)))
    for j in range(CH):
        sa[pl.ds(j, 16, stride=REC), :] = chunk(gathered, j)
        sa[pl.ds(CH + j, 16, stride=REC), :] = chunk(backs, j)
    sa[pl.ds(20, 16, stride=REC), :] = jnp.broadcast_to(peak, (16, 128))
    sa[pl.ds(21, 16, stride=REC), :] = jnp.broadcast_to(total, (16, 128))
    for i in (22, 23):
        sa[pl.ds(i, 16, stride=REC), :] = jnp.zeros((16, 128), F32)
    halves[pl.ds(PAIR, 8), :] = jnp.zeros((8, 128), F32)
    loads[3].wait()
    router = core_major(router_v[...].astype(F32))
    loads[4].wait()
    loads[5].wait()

    @pl.when(core == 0)
    def _():
        pl.semaphore_wait(near_sem, 1)

    send(0, sa.at[pl.ds((1 - core) * 192, 192)], ra, sibling)
    wait(recv_sem.at[0], ra)
    own = sa[pl.ds(pl.multiple_of(core * 192, 192), 192), :].reshape(8, REC, 128)
    other = ra[...].reshape(8, REC, 128)
    scaled = (row < CH) | (row == 21)
    top = jnp.maximum(own[:, 20:21, :], other[:, 20:21, :])
    both = own * jnp.where(scaled, jnp.exp(own[:, 20:21, :] - top), 1.0) + other * jnp.where(
        scaled, jnp.exp(other[:, 20:21, :] - top), 1.0
    )
    count = both[:, 21:22, :]
    both = jnp.where(row == 20, top, jnp.where(row == 22, count - low(count), both))
    sz[...] = both.astype(BF16)
    rz[pl.ds(z, 1)] = sz[pl.ds(zlo, 1)]

    @pl.when(core == 0)
    def _():
        pl.semaphore_wait(barrier, 60)
        pl.semaphore_signal(far_sem, inc=1, device_id=sibling, device_id_type=MESH)

    @pl.when(core == 1)
    def _():
        pl.semaphore_wait(far_sem, 1)

    for z_to in z_peers:
        send(1, sz.at[lax.rem(z_to, 8)], rz.at[z], device(z_to, xy, core))
    wait(recv_sem.at[1], rz.at[pl.ds(0, ZN - 1)])
    slots, tops, totals = [], [], []
    for h in range(2):
        part = rz[pl.ds(8 * h, 8)].astype(F32)
        peaks = part[:, 20:21, :]
        top = jnp.max(peaks, axis=0)
        factor = jnp.exp(peaks - top)
        count = jnp.sum(factor * (part[:, 21:22, :] + part[:, 22:23, :]), axis=0)
        summed = jnp.sum(part * jnp.where(row < CH, factor, 1.0), axis=0)
        slots.append(jnp.where(row < CH, summed / count, summed))
        tops.append(top)
        totals.append(count)
        sb[pl.ds(2 * CH * h, 2 * CH), :] = slots[h][: 2 * CH]
    packed = sb[...].astype(BF16)
    rb[pl.ds(xy, 1)] = packed[None]

    for xy_to in xy_peers:
        send(2, rb.at[xy], rb.at[xy], device(z, xy_to, core))
    wait(recv_sem.at[2], rb.at[pl.ds(0, XYN - 1)])
    wide[...] = rb[...].astype(F32).reshape(XYN * PAIR, 128)

    def clips(first):
        return jnp.concatenate(
            [
                jnp.concatenate(
                    [wide[pl.ds(h * 2 * CH + first + j, 16, stride=PAIR), :].astype(BF16) for j in range(CH)],
                    axis=1,
                )
                for h in range(2)
            ],
            axis=0,
        )

    every_in, every_back = clips(0), clips(CH)
    pre = dot(every_in, w_in_v[0], ((1,), (1,)))
    act_back = dot(every_back, w_out_v[0], ((1,), (1,)))
    slope = math.sqrt(2.0 / math.pi)
    bent = jnp.tanh(slope * (pre + 0.044715 * (pre * pre * pre)))
    activated = (0.5 * pre * (1.0 + bent)).astype(BF16)
    gelu_slope = 0.5 * (1.0 + bent) + 0.5 * pre * ((1.0 + bent) * (1.0 - bent)) * (
        slope * (1.0 + 3.0 * 0.044715 * (pre * pre))
    )
    hidden_back = (gelu_slope * act_back).astype(BF16)
    in_part = dot(hidden_back, w_in_v[0], ((1,), (0,)))
    out_part = dot(activated, w_out_v[0], ((1,), (0,)))
    for h in range(2):
        for j in range(CH):
            wide[pl.ds(h * 2 * CH + j, 16, stride=PAIR), :] = chunk(in_part, j)[16 * h : 16 * h + 16]
            wide[pl.ds(h * 2 * CH + CH + j, 16, stride=PAIR), :] = chunk(out_part, j)[16 * h : 16 * h + 16]
    sc[...] = wide[...].reshape(XYN, PAIR, 128).astype(BF16)
    rc[pl.ds(xy, 1)] = sc[pl.ds(xy, 1)]

    for xy_to in xy_peers:
        send(3, sc.at[xy_to], rc.at[xy], device(z, xy_to, core))
    w_out_grad_v[0] = dot(activated, every_back, ((0,), (0,))).astype(BF16)
    w_in_grad_v[0] = dot(hidden_back, every_in, ((0,), (0,))).astype(BF16)
    stores = [
        pltpu.make_async_copy(w_in_grad_v, w_in_grad_hbm, out_sem.at[0]),
        pltpu.make_async_copy(w_out_grad_v, w_out_grad_hbm, out_sem.at[1]),
        pltpu.make_async_copy(token_grad_v, token_grad_hbm, out_sem.at[2]),
        pltpu.make_async_copy(router_grad_ref, router_grad_hbm, out_sem.at[3]),
    ]
    stores[0].start()
    stores[1].start()
    wait(recv_sem.at[3], rc.at[pl.ds(0, XYN - 1)])
    halves[pl.ds(0, PAIR), :] = jnp.sum(rc[...].astype(F32), axis=0)
    for h in range(2):
        half = halves[pl.ds(2 * CH * h, REC), :]
        dotted = jnp.sum(jnp.where(row < CH, low(half) * slots[h], 0.0), keepdims=True)
        half = jnp.where(row == 20, tops[h], half)
        half = jnp.where(row == 21, totals[h], half)
        half = jnp.where(row == 22, totals[h] - low(totals[h]), half)
        half = jnp.where(row == 23, jnp.where(lane < 64, dotted, dotted - low(dotted)), half)
        sd[pl.ds(h, 1)] = half.astype(BF16)[None]
    rd[pl.ds(z, 1)] = sd[pl.ds(zhi, 1)]

    for z_to in z_peers:
        send(4, sd.at[z_to // 8], rd.at[z], device(z_to, xy, core))
    wait(recv_sem.at[4], rd.at[pl.ds(0, ZN - 1)])
    first, second = rd[pl.ds(0, 8)].astype(F32), rd[pl.ds(8, 8)].astype(F32)
    both = first + second
    dotted = both[:, 23:24, 0:1] + both[:, 23:24, 64:65]
    both = jnp.where(row == 20, first, both)
    both = jnp.where(row == 21, first[:, 21:22, :] + first[:, 22:23, :], both)
    both = jnp.where(row == 23, dotted, both)
    mine = pl.ds(pl.multiple_of(core * 192, 192), 192)
    se[mine, :] = both.reshape(192, 128)

    send(5, se.at[mine], se.at[mine], sibling)
    wait(recv_sem.at[5], ra)

    def slot_rows(first):
        return jnp.concatenate([se[pl.ds(first + j, 16, stride=REC), :] for j in range(CH)], axis=1).astype(BF16)

    in_back, slot_out = slot_rows(0), slot_rows(CH)
    col_peak = se[pl.ds(20, 16, stride=REC), :][:, 0:1]
    col_total = se[pl.ds(21, 16, stride=REC), :][:, 0:1]
    slot_total = se[pl.ds(23, 16, stride=REC), :][:, 0:1]
    dispatch = (jnp.exp(logits - col_peak) / col_total).astype(BF16)
    weights = dispatch.astype(F32)
    combine_back = dot(slot_out, grads_v[0], ((1,), (1,)))
    dispatch_back = dot(in_back, tokens_v[0], ((1,), (1,)))
    logit_comb = combine * (combine_back - jnp.sum(combine * combine_back, axis=0, keepdims=True))
    logit_back = (logit_comb + weights * (dispatch_back - slot_total)).astype(BF16)
    router_part = dot(logit_back, tokens_v[0], ((1,), (0,)))
    for j in range(CH):
        rows[pl.ds(j, 16, stride=16), :] = chunk(router_part, j)
    for j in range(CH, 16):
        rows[pl.ds(j, 16, stride=16), :] = jnp.zeros((16, 128), F32)
    sf[...] = rows[...].reshape(16, 16, 128).astype(BF16)
    rf[pl.ds(xy, 1)] = sf[pl.ds(xy, 1)]

    for xy_to in xy_peers:
        send(6, sf.at[xy_to], rf.at[xy], device(z, xy_to, core))
    left = jnp.concatenate([weights, logit_back.astype(F32)], axis=0).astype(BF16)
    right = jnp.concatenate([in_back.astype(F32), router], axis=0).astype(BF16)
    token_grad_v[0] = (dot(left, right, ((0,), (0,))) * 64.0).astype(BF16)
    stores[2].start()
    wait(recv_sem.at[6], rf.at[pl.ds(0, XYN - 1)])
    sh[...] = jnp.sum(rf[...].astype(F32), axis=0).astype(BF16)
    rh[pl.ds(z, 1)] = sh[...][None]

    for z_to in z_peers:
        send(7, sh, rh.at[z], device(z_to, xy, core))
    wait(recv_sem.at[7], rh.at[pl.ds(0, ZN - 1)])
    place = core * 16 + lax.rem(xy, 8) * 2 + xy // 8
    ri[pl.ds(place, 1)] = jnp.sum(rh[...].astype(F32), axis=0).astype(BF16)[None]

    for xy_to in xy_peers:
        send(8, ri.at[place], ri.at[place], device(z, xy_to, core))
        send(8, ri.at[place], ri.at[place], device(z, xy_to, 1 - core))
    send(8, ri.at[place], ri.at[place], sibling)
    wait(recv_sem.at[8], ri.at[pl.ds(0, 31)])
    rows[...] = ((ri[pl.ds(0, 16)].astype(F32) + ri[pl.ds(16, 16)].astype(F32)) / math.sqrt(32.0)).reshape(256, 128)
    for j in range(CH):
        router_grad_ref[:, j * 128 : (j + 1) * 128] = rows[pl.ds(j, 16, stride=16), :]
    stores[3].start()

    wait(send_sem.at[0], ra)
    wait(send_sem.at[1], rz.at[pl.ds(0, ZN - 1)])
    wait(send_sem.at[2], rb.at[pl.ds(0, XYN - 1)])
    wait(send_sem.at[3], rc.at[pl.ds(0, XYN - 1)])
    wait(send_sem.at[4], rd.at[pl.ds(0, ZN - 1)])
    wait(send_sem.at[5], ra)
    wait(send_sem.at[6], rf.at[pl.ds(0, XYN - 1)])
    wait(send_sem.at[7], rh.at[pl.ds(0, ZN - 1)])
    wait(send_sem.at[8], ri.at[pl.ds(0, 31)])
    for copy in stores:
        copy.wait()


def store_kernel(*refs):
    sources, targets, sems = refs[:4], refs[4:8], refs[8]
    copies = []
    for a, b in zip(sources, targets):
        if len(a.shape) == 2:
            parts = [(a, b)]
        else:
            cut = a.shape[1] // 2
            parts = [(a.at[:, pl.ds(i * cut, cut)], b.at[:, pl.ds(i * cut, cut)]) for i in range(2)]
        for part, to in parts:
            copies.append(pltpu.make_async_copy(part, to, sems.at[len(copies)]))
            copies[-1].start()
    for copy in copies:
        copy.wait()


def local(tokens, out_grad, logits, router, w_in, w_out):
    anywhere = pl.BlockSpec(memory_space=pl.ANY)
    hbm = pl.BlockSpec(memory_space=pltpu.HBM)
    w_in = jnp.swapaxes(w_in, 1, 2)
    inputs = tuple(
        pltpu.with_memory_space_constraint(a, pltpu.HBM) for a in (tokens, out_grad, logits, router, w_in, w_out)
    )
    results = (
        jax.ShapeDtypeStruct(tokens.shape, BF16),
        jax.ShapeDtypeStruct(router.shape, F32),
        jax.ShapeDtypeStruct(w_in.shape, BF16),
        jax.ShapeDtypeStruct(w_out.shape, BF16),
    )
    made = pl.pallas_call(
        kernel,
        name="moe_back",
        out_shape=tuple(pltpu.VMEM(a.shape, a.dtype) for a in results),
        in_specs=[hbm] * 6,
        out_specs=(anywhere,) * 4,
        scratch_shapes=[pltpu.VMEM(a.shape, a.dtype) for a in inputs]
        + [
            pltpu.VMEM(tokens.shape, BF16),
            pltpu.VMEM(router.shape, F32),
            pltpu.VMEM(w_in.shape, BF16),
            pltpu.VMEM(w_out.shape, BF16),
            pltpu.VMEM((16 * REC, 128), F32),
            pltpu.VMEM((8 * REC, 128), F32),
            pltpu.VMEM((8, REC, 128), BF16),
            pltpu.VMEM((ZN, REC, 128), BF16),
            pltpu.VMEM((PAIR, 128), F32),
            pltpu.VMEM((XYN, PAIR, 128), BF16),
            pltpu.VMEM((XYN * PAIR, 128), F32),
            pltpu.VMEM((XYN, PAIR, 128), BF16),
            pltpu.VMEM((XYN, PAIR, 128), BF16),
            pltpu.VMEM((48, 128), F32),
            pltpu.VMEM((2, REC, 128), BF16),
            pltpu.VMEM((ZN, REC, 128), BF16),
            pltpu.VMEM((16 * REC, 128), F32),
            pltpu.VMEM((16 * 16, 128), F32),
            pltpu.VMEM((16, 16, 128), BF16),
            pltpu.VMEM((XYN, 16, 128), BF16),
            pltpu.VMEM((16, 128), BF16),
            pltpu.VMEM((ZN, 16, 128), BF16),
            pltpu.VMEM((2 * 16, 16, 128), BF16),
            pltpu.SemaphoreType.DMA((6,)),
            pltpu.SemaphoreType.DMA((4,)),
            pltpu.SemaphoreType.DMA((9,)),
            pltpu.SemaphoreType.DMA((9,)),
            pltpu.SemaphoreType.REGULAR,
            pltpu.SemaphoreType.REGULAR,
        ],
        compiler_params=pltpu.CompilerParams(
            collective_id=0, has_side_effects=True, vmem_limit_bytes=32 * 1024 * 1024
        ),
    )(*inputs)
    token_grad, router_grad, w_in_grad, w_out_grad = pl.pallas_call(
        store_kernel,
        name="store",
        out_shape=results,
        in_specs=[anywhere] * 4,
        out_specs=(hbm,) * 4,
        scratch_shapes=[pltpu.SemaphoreType.DMA((7,))],
    )(*(pltpu.with_memory_space_constraint(a, pltpu.VMEM) for a in made))
    return (token_grad, router_grad, jnp.swapaxes(w_in_grad, 1, 2), w_out_grad)


def solution(mesh):
    return jax.shard_map(
        local,
        mesh=mesh,
        in_specs=(
            P("dp", "seq", None),
            P("dp", "seq", None),
            P("dp", None, "seq"),
            P(),
            P("seq", None, "dp"),
            P("seq", "dp", None),
        ),
        out_specs=(P("dp", "seq", None), P(), P("seq", None, "dp"), P("seq", "dp", None)),
        check_vma=False,
    )
```

```python
import functools
import math

import jax
import jax.numpy as jnp
from jax import lax
from jax.experimental import pallas as pl
from jax.experimental.pallas import tpu as pltpu
from jax.sharding import PartitionSpec as P

MESH = pl.DeviceIdType.MESH
F32 = jnp.float32
BF16 = jnp.bfloat16

D = 1280
CH = D // 128
PAIR = 4 * CH
REC = 24
ZN = 16
XYN = 16
Z_ORDER = (8, 7, 9, 6, 10, 5, 11, 4, 12, 3, 13, 2, 14, 1, 15)
XY_ORDER = (
    (2, 2), (2, 1), (2, 3), (1, 2), (3, 2), (1, 1), (1, 3), (3, 1), (3, 3), (2, 0), (0, 2), (1, 0), (3, 0), (0, 1), (0, 3),
)


def low(value):
    return value.astype(BF16).astype(F32)


def dot(left, right, dims):
    return lax.dot_general(left, right, (dims, ((), ())), preferred_element_type=F32)


def kernel(
    tokens_hbm, grads_hbm, logits_hbm, router_hbm, w_in_hbm, w_out_hbm,
    token_grad_hbm, router_grad_hbm, w_in_grad_hbm, w_out_grad_hbm,
    tokens_v, grads_v, logits_v, router_v, w_in_v, w_out_v, token_grad_v, router_grad_ref, w_in_grad_v, w_out_grad_v,
    sa, ra, sz, rz, sb, rb, wide, sc, rc, halves, sd, rd, se, rows, sf, rf, sh, rh, ri,
    in_sem, out_sem, send_sem, recv_sem, near_sem, far_sem,
):
    dp, sq = lax.axis_index("dp"), lax.axis_index("seq")
    zhi, xy = dp // 16, lax.rem(dp, 16)
    zlo, core = sq // 2, lax.rem(sq, 2)
    z = zhi * 8 + zlo
    x, y = xy // 4, lax.rem(xy, 4)

    def device(z_to, xy_to, core_to):
        return (z_to // 8 * 16 + xy_to, lax.rem(z_to, 8) * 2 + core_to)

    z_peers = [lax.rem(z + k, ZN) for k in Z_ORDER]
    xy_peers = [lax.rem(x + dx, 4) * 4 + lax.rem(y + dy, 4) for dx, dy in XY_ORDER]
    sibling = device(z, xy, 1 - core)

    barrier = pltpu.get_barrier_semaphore()

    @pl.when(core == 1)
    def _():
        pl.semaphore_signal(barrier, inc=1, device_id=sibling, device_id_type=MESH)

    for z_to in z_peers:
        pl.semaphore_signal(barrier, inc=1, device_id=device(z_to, xy, 1), device_id_type=MESH)
    for xy_to in xy_peers:
        pl.semaphore_signal(barrier, inc=1, device_id=device(z, xy_to, 1), device_id_type=MESH)

    loads = []
    for i, (src, dst) in enumerate(
        (
            (logits_hbm, logits_v),
            (tokens_hbm, tokens_v),
            (grads_hbm, grads_v),
            (router_hbm, router_v),
            (w_in_hbm, w_in_v),
            (w_out_hbm, w_out_v),
        )
    ):
        copy = pltpu.make_async_copy(src, dst, in_sem.at[i])
        copy.start()
        loads.append(copy)

    @pl.when(core == 0)
    def _():
        pl.semaphore_wait(barrier, 1)
        pl.semaphore_signal(near_sem, inc=1, device_id=sibling, device_id_type=MESH)

    def send(stage, src, dst, to):
        pltpu.make_async_remote_copy(
            src_ref=src,
            dst_ref=dst,
            send_sem=send_sem.at[stage],
            recv_sem=recv_sem.at[stage],
            device_id=to,
            device_id_type=MESH,
        ).start()

    def wait(sem, ref):
        pltpu.make_async_copy(ref, ref, sem).wait()

    row = lax.broadcasted_iota(jnp.int32, (REC, 128), 0)
    lane = lax.broadcasted_iota(jnp.int32, (REC, 128), 1)

    def chunk(value, j):
        return value[:, j * 128 : (j + 1) * 128]

    def core_major(rows):
        return jnp.concatenate([rows[2 * j + p : 2 * j + p + 1] for p in range(2) for j in range(8)], axis=0)

    loads[0].wait()
    logits = core_major(logits_v[0])
    raised_c = jnp.exp(logits - jnp.max(logits, axis=0, keepdims=True))
    combine = raised_c / jnp.sum(raised_c, axis=0, keepdims=True)
    peak = low(jnp.max(logits, axis=1, keepdims=True))
    raised = jnp.exp(logits - peak)
    total = jnp.sum(raised, axis=1, keepdims=True)
    loads[1].wait()
    gathered = dot(raised.astype(BF16), tokens_v[0], ((1,), (0,)))
    loads[2].wait()
    backs = dot(combine.astype(BF16), grads_v[0], ((1,), (0,)))
    for j in range(CH):
        sa[pl.ds(j, 16, stride=REC), :] = chunk(gathered, j)
        sa[pl.ds(CH + j, 16, stride=REC), :] = chunk(backs, j)
    sa[pl.ds(20, 16, stride=REC), :] = jnp.broadcast_to(peak, (16, 128))
    sa[pl.ds(21, 16, stride=REC), :] = jnp.broadcast_to(total, (16, 128))
    for i in (22, 23):
        sa[pl.ds(i, 16, stride=REC), :] = jnp.zeros((16, 128), F32)
    halves[pl.ds(PAIR, 8), :] = jnp.zeros((8, 128), F32)
    loads[3].wait()
    router = core_major(router_v[...].astype(F32))
    loads[4].wait()
    loads[5].wait()

    @pl.when(core == 1)
    def _():
        pl.semaphore_wait(near_sem, 1)

    send(0, sa.at[pl.ds((1 - core) * 192, 192)], ra, sibling)
    wait(recv_sem.at[0], ra)
    own = sa[pl.ds(pl.multiple_of(core * 192, 192), 192), :].reshape(8, REC, 128)
    other = ra[...].reshape(8, REC, 128)
    scaled = (row < CH) | (row == 21)
    top = jnp.maximum(own[:, 20:21, :], other[:, 20:21, :])
    both = own * jnp.where(scaled, jnp.exp(own[:, 20:21, :] - top), 1.0) + other * jnp.where(
        scaled, jnp.exp(other[:, 20:21, :] - top), 1.0
    )
    count = both[:, 21:22, :]
    both = jnp.where(row == 20, top, jnp.where(row == 22, count - low(count), both))
    sz[...] = both.astype(BF16)
    rz[pl.ds(z, 1)] = sz[pl.ds(zlo, 1)]

    @pl.when(core == 1)
    def _():
        pl.semaphore_wait(barrier, 60)
        pl.semaphore_signal(far_sem, inc=1, device_id=sibling, device_id_type=MESH)

    @pl.when(core == 0)
    def _():
        pl.semaphore_wait(far_sem, 1)

    for z_to in z_peers:
        send(1, sz.at[lax.rem(z_to, 8)], rz.at[z], device(z_to, xy, core))
    wait(recv_sem.at[1], rz.at[pl.ds(0, ZN - 1)])
    slots, tops, totals = [], [], []
    for h in range(2):
        part = rz[pl.ds(8 * h, 8)].astype(F32)
        peaks = part[:, 20:21, :]
        top = jnp.max(peaks, axis=0)
        factor = jnp.exp(peaks - top)
        count = jnp.sum(factor * (part[:, 21:22, :] + part[:, 22:23, :]), axis=0)
        summed = jnp.sum(part * jnp.where(row < CH, factor, 1.0), axis=0)
        slots.append(jnp.where(row < CH, summed / count, summed))
        tops.append(top)
        totals.append(count)
        sb[pl.ds(2 * CH * h, 2 * CH), :] = slots[h][: 2 * CH]
    packed = sb[...].astype(BF16)
    rb[pl.ds(xy, 1)] = packed[None]

    for xy_to in xy_peers:
        send(2, rb.at[xy], rb.at[xy], device(z, xy_to, core))
    wait(recv_sem.at[2], rb.at[pl.ds(0, XYN - 1)])
    wide[...] = rb[...].astype(F32).reshape(XYN * PAIR, 128)

    def clips(first):
        return jnp.concatenate(
            [
                jnp.concatenate(
                    [wide[pl.ds(h * 2 * CH + first + j, 16, stride=PAIR), :].astype(BF16) for j in range(CH)],
                    axis=1,
                )
                for h in range(2)
            ],
            axis=0,
        )

    every_in, every_back = clips(0), clips(CH)
    pre = dot(every_in, w_in_v[0], ((1,), (1,)))
    act_back = dot(every_back, w_out_v[0], ((1,), (1,)))
    slope = math.sqrt(2.0 / math.pi)
    bent = jnp.tanh(slope * (pre + 0.044715 * (pre * pre * pre)))
    activated = (0.5 * pre * (1.0 + bent)).astype(BF16)
    gelu_slope = 0.5 * (1.0 + bent) + 0.5 * pre * ((1.0 + bent) * (1.0 - bent)) * (
        slope * (1.0 + 3.0 * 0.044715 * (pre * pre))
    )
    hidden_back = (gelu_slope * act_back).astype(BF16)
    in_part = dot(hidden_back, w_in_v[0], ((1,), (0,)))
    out_part = dot(activated, w_out_v[0], ((1,), (0,)))
    for h in range(2):
        for j in range(CH):
            wide[pl.ds(h * 2 * CH + j, 16, stride=PAIR), :] = chunk(in_part, j)[16 * h : 16 * h + 16]
            wide[pl.ds(h * 2 * CH + CH + j, 16, stride=PAIR), :] = chunk(out_part, j)[16 * h : 16 * h + 16]
    sc[...] = wide[...].reshape(XYN, PAIR, 128).astype(BF16)
    rc[pl.ds(xy, 1)] = sc[pl.ds(xy, 1)]

    for xy_to in xy_peers:
        send(3, sc.at[xy_to], rc.at[xy], device(z, xy_to, core))
    w_out_grad_v[0] = dot(activated, every_back, ((0,), (0,))).astype(BF16)
    w_in_grad_v[0] = dot(hidden_back, every_in, ((0,), (0,))).astype(BF16)
    stores = [
        pltpu.make_async_copy(w_in_grad_v, w_in_grad_hbm, out_sem.at[0]),
        pltpu.make_async_copy(w_out_grad_v, w_out_grad_hbm, out_sem.at[1]),
        pltpu.make_async_copy(token_grad_v, token_grad_hbm, out_sem.at[2]),
        pltpu.make_async_copy(router_grad_ref, router_grad_hbm, out_sem.at[3]),
    ]
    stores[0].start()
    stores[1].start()
    wait(recv_sem.at[3], rc.at[pl.ds(0, XYN - 1)])
    halves[pl.ds(0, PAIR), :] = jnp.sum(rc[...].astype(F32), axis=0)
    for h in range(2):
        half = halves[pl.ds(2 * CH * h, REC), :]
        dotted = jnp.sum(jnp.where(row < CH, low(half) * slots[h], 0.0), keepdims=True)
        half = jnp.where(row == 20, tops[h], half)
        half = jnp.where(row == 21, totals[h], half)
        half = jnp.where(row == 22, totals[h] - low(totals[h]), half)
        half = jnp.where(row == 23, jnp.where(lane < 64, dotted, dotted - low(dotted)), half)
        sd[pl.ds(h, 1)] = half.astype(BF16)[None]
    rd[pl.ds(z, 1)] = sd[pl.ds(zhi, 1)]

    for z_to in z_peers:
        send(4, sd.at[z_to // 8], rd.at[z], device(z_to, xy, core))
    wait(recv_sem.at[4], rd.at[pl.ds(0, ZN - 1)])
    first, second = rd[pl.ds(0, 8)].astype(F32), rd[pl.ds(8, 8)].astype(F32)
    both = first + second
    dotted = both[:, 23:24, 0:1] + both[:, 23:24, 64:65]
    both = jnp.where(row == 20, first, both)
    both = jnp.where(row == 21, first[:, 21:22, :] + first[:, 22:23, :], both)
    both = jnp.where(row == 23, dotted, both)
    mine = pl.ds(pl.multiple_of(core * 192, 192), 192)
    se[mine, :] = both.reshape(192, 128)

    send(5, se.at[mine], se.at[mine], sibling)
    wait(recv_sem.at[5], ra)

    def slot_rows(first):
        return jnp.concatenate([se[pl.ds(first + j, 16, stride=REC), :] for j in range(CH)], axis=1).astype(BF16)

    in_back, slot_out = slot_rows(0), slot_rows(CH)
    col_peak = se[pl.ds(20, 16, stride=REC), :][:, 0:1]
    col_total = se[pl.ds(21, 16, stride=REC), :][:, 0:1]
    slot_total = se[pl.ds(23, 16, stride=REC), :][:, 0:1]
    dispatch = (jnp.exp(logits - col_peak) / col_total).astype(BF16)
    weights = dispatch.astype(F32)
    combine_back = dot(slot_out, grads_v[0], ((1,), (1,)))
    dispatch_back = dot(in_back, tokens_v[0], ((1,), (1,)))
    logit_comb = combine * (combine_back - jnp.sum(combine * combine_back, axis=0, keepdims=True))
    logit_back = (logit_comb + weights * (dispatch_back - slot_total)).astype(BF16)
    router_part = dot(logit_back, tokens_v[0], ((1,), (0,)))
    for j in range(CH):
        rows[pl.ds(j, 16, stride=16), :] = chunk(router_part, j)
    for j in range(CH, 16):
        rows[pl.ds(j, 16, stride=16), :] = jnp.zeros((16, 128), F32)
    sf[...] = rows[...].reshape(16, 16, 128).astype(BF16)
    rf[pl.ds(xy, 1)] = sf[pl.ds(xy, 1)]

    for xy_to in xy_peers:
        send(6, sf.at[xy_to], rf.at[xy], device(z, xy_to, core))
    left = jnp.concatenate([weights, logit_back.astype(F32)], axis=0).astype(BF16)
    right = jnp.concatenate([in_back.astype(F32), router], axis=0).astype(BF16)
    token_grad_v[0] = (dot(left, right, ((0,), (0,))) * 64.0).astype(BF16)
    stores[2].start()
    wait(recv_sem.at[6], rf.at[pl.ds(0, XYN - 1)])
    sh[...] = jnp.sum(rf[...].astype(F32), axis=0).astype(BF16)
    rh[pl.ds(z, 1)] = sh[...][None]

    for z_to in z_peers:
        send(7, sh, rh.at[z], device(z_to, xy, core))
    wait(recv_sem.at[7], rh.at[pl.ds(0, ZN - 1)])
    place = core * 16 + lax.rem(xy, 8) * 2 + xy // 8
    ri[pl.ds(place, 1)] = jnp.sum(rh[...].astype(F32), axis=0).astype(BF16)[None]

    for xy_to in xy_peers:
        send(8, ri.at[place], ri.at[place], device(z, xy_to, core))
        send(8, ri.at[place], ri.at[place], device(z, xy_to, 1 - core))
    send(8, ri.at[place], ri.at[place], sibling)
    wait(recv_sem.at[8], ri.at[pl.ds(0, 31)])
    rows[...] = ((ri[pl.ds(0, 16)].astype(F32) + ri[pl.ds(16, 16)].astype(F32)) / math.sqrt(32.0)).reshape(256, 128)
    for j in range(CH):
        router_grad_ref[:, j * 128 : (j + 1) * 128] = rows[pl.ds(j, 16, stride=16), :]
    stores[3].start()

    wait(send_sem.at[0], ra)
    wait(send_sem.at[1], rz.at[pl.ds(0, ZN - 1)])
    wait(send_sem.at[2], rb.at[pl.ds(0, XYN - 1)])
    wait(send_sem.at[3], rc.at[pl.ds(0, XYN - 1)])
    wait(send_sem.at[4], rd.at[pl.ds(0, ZN - 1)])
    wait(send_sem.at[5], ra)
    wait(send_sem.at[6], rf.at[pl.ds(0, XYN - 1)])
    wait(send_sem.at[7], rh.at[pl.ds(0, ZN - 1)])
    wait(send_sem.at[8], ri.at[pl.ds(0, 31)])
    for copy in stores:
        copy.wait()


def store_kernel(*refs):
    sources, targets, sems = refs[:4], refs[4:8], refs[8]
    copies = []
    for a, b in zip(sources, targets):
        if len(a.shape) == 2:
            parts = [(a, b)]
        else:
            cut = a.shape[1] // 2
            parts = [(a.at[:, pl.ds(i * cut, cut)], b.at[:, pl.ds(i * cut, cut)]) for i in range(2)]
        for part, to in parts:
            copies.append(pltpu.make_async_copy(part, to, sems.at[len(copies)]))
            copies[-1].start()
    for copy in copies:
        copy.wait()


def local(tokens, out_grad, logits, router, w_in, w_out):
    anywhere = pl.BlockSpec(memory_space=pl.ANY)
    hbm = pl.BlockSpec(memory_space=pltpu.HBM)
    w_in = jnp.swapaxes(w_in, 1, 2)
    inputs = tuple(
        pltpu.with_memory_space_constraint(a, pltpu.HBM) for a in (tokens, out_grad, logits, router, w_in, w_out)
    )
    results = (
        jax.ShapeDtypeStruct(tokens.shape, BF16),
        jax.ShapeDtypeStruct(router.shape, F32),
        jax.ShapeDtypeStruct(w_in.shape, BF16),
        jax.ShapeDtypeStruct(w_out.shape, BF16),
    )
    made = pl.pallas_call(
        kernel,
        name="moe_back",
        out_shape=tuple(pltpu.VMEM(a.shape, a.dtype) for a in results),
        in_specs=[hbm] * 6,
        out_specs=(anywhere,) * 4,
        scratch_shapes=[pltpu.VMEM(a.shape, a.dtype) for a in inputs]
        + [
            pltpu.VMEM(tokens.shape, BF16),
            pltpu.VMEM(router.shape, F32),
            pltpu.VMEM(w_in.shape, BF16),
            pltpu.VMEM(w_out.shape, BF16),
            pltpu.VMEM((16 * REC, 128), F32),
            pltpu.VMEM((8 * REC, 128), F32),
            pltpu.VMEM((8, REC, 128), BF16),
            pltpu.VMEM((ZN, REC, 128), BF16),
            pltpu.VMEM((PAIR, 128), F32),
            pltpu.VMEM((XYN, PAIR, 128), BF16),
            pltpu.VMEM((XYN * PAIR, 128), F32),
            pltpu.VMEM((XYN, PAIR, 128), BF16),
            pltpu.VMEM((XYN, PAIR, 128), BF16),
            pltpu.VMEM((48, 128), F32),
            pltpu.VMEM((2, REC, 128), BF16),
            pltpu.VMEM((ZN, REC, 128), BF16),
            pltpu.VMEM((16 * REC, 128), F32),
            pltpu.VMEM((16 * 16, 128), F32),
            pltpu.VMEM((16, 16, 128), BF16),
            pltpu.VMEM((XYN, 16, 128), BF16),
            pltpu.VMEM((16, 128), BF16),
            pltpu.VMEM((ZN, 16, 128), BF16),
            pltpu.VMEM((2 * 16, 16, 128), BF16),
            pltpu.SemaphoreType.DMA((6,)),
            pltpu.SemaphoreType.DMA((4,)),
            pltpu.SemaphoreType.DMA((9,)),
            pltpu.SemaphoreType.DMA((9,)),
            pltpu.SemaphoreType.REGULAR,
            pltpu.SemaphoreType.REGULAR,
        ],
        compiler_params=pltpu.CompilerParams(
            collective_id=0, has_side_effects=True, vmem_limit_bytes=32 * 1024 * 1024
        ),
    )(*inputs)
    token_grad, router_grad, w_in_grad, w_out_grad = pl.pallas_call(
        store_kernel,
        name="store",
        out_shape=results,
        in_specs=[anywhere] * 4,
        out_specs=(hbm,) * 4,
        scratch_shapes=[pltpu.SemaphoreType.DMA((7,))],
    )(*(pltpu.with_memory_space_constraint(a, pltpu.VMEM) for a in made))
    return (token_grad, router_grad, jnp.swapaxes(w_in_grad, 1, 2), w_out_grad)


def solution(mesh):
    return jax.shard_map(
        local,
        mesh=mesh,
        in_specs=(
            P("dp", "seq", None),
            P("dp", "seq", None),
            P("dp", None, "seq"),
            P(),
            P("seq", None, "dp"),
            P("seq", "dp", None),
        ),
        out_specs=(P("dp", "seq", None), P(), P("seq", None, "dp"), P("seq", "dp", None)),
        check_vma=False,
    )
```

```python
import functools
import math

import jax
import jax.numpy as jnp
from jax import lax
from jax.experimental import pallas as pl
from jax.experimental.pallas import tpu as pltpu
from jax.sharding import PartitionSpec as P

MESH = pl.DeviceIdType.MESH
F32 = jnp.float32
BF16 = jnp.bfloat16

D = 1280
CH = D // 128
PAIR = 4 * CH
REC = 24
ZN = 16
XYN = 16
Z_ORDER = (8, 7, 9, 6, 10, 5, 11, 4, 12, 3, 13, 2, 14, 1, 15)
XY_ORDER = (
    (2, 2), (2, 1), (2, 3), (1, 2), (3, 2), (1, 1), (1, 3), (3, 1), (3, 3), (2, 0), (0, 2), (1, 0), (3, 0), (0, 1), (0, 3),
)


def low(value):
    return value.astype(BF16).astype(F32)


def dot(left, right, dims):
    return lax.dot_general(left, right, (dims, ((), ())), preferred_element_type=F32)


def kernel(
    tokens_hbm, grads_hbm, logits_hbm, router_hbm, w_in_hbm, w_out_hbm,
    token_grad_hbm, ri, w_in_grad_hbm, w_out_grad_hbm,
    tokens_v, grads_v, logits_v, router_v, w_in_v, w_out_v, token_grad_v, w_in_grad_v, w_out_grad_v,
    sa, ra, sz, rz, sb, rb, wide, sc, rc, halves, sd, rd, se, rows, sf, rf, own_row, other_row, sh, rh, summed_row,
    in_sem, out_sem, send_sem, recv_sem, near_sem, far_sem,
):
    dp, sq = lax.axis_index("dp"), lax.axis_index("seq")
    zhi, xy = dp // 16, lax.rem(dp, 16)
    zlo, core = sq // 2, lax.rem(sq, 2)
    z = zhi * 8 + zlo
    x, y = xy // 4, lax.rem(xy, 4)

    def device(z_to, xy_to, core_to):
        return (z_to // 8 * 16 + xy_to, lax.rem(z_to, 8) * 2 + core_to)

    z_peers = [lax.rem(z + k, ZN) for k in Z_ORDER]
    xy_peers = [lax.rem(x + dx, 4) * 4 + lax.rem(y + dy, 4) for dx, dy in XY_ORDER]
    sibling = device(z, xy, 1 - core)

    barrier = pltpu.get_barrier_semaphore()

    @pl.when(core == 1)
    def _():
        pl.semaphore_signal(barrier, inc=1, device_id=sibling, device_id_type=MESH)

    for z_to in z_peers:
        pl.semaphore_signal(barrier, inc=1, device_id=device(z_to, xy, 1), device_id_type=MESH)
    for xy_to in xy_peers:
        pl.semaphore_signal(barrier, inc=1, device_id=device(z, xy_to, 1), device_id_type=MESH)

    loads = []
    for i, (src, dst) in enumerate(
        (
            (logits_hbm, logits_v),
            (tokens_hbm, tokens_v),
            (grads_hbm, grads_v),
            (router_hbm, router_v),
            (w_in_hbm, w_in_v),
            (w_out_hbm, w_out_v),
        )
    ):
        copy = pltpu.make_async_copy(src, dst, in_sem.at[i])
        copy.start()
        loads.append(copy)

    @pl.when(core == 0)
    def _():
        pl.semaphore_wait(barrier, 1)
        pl.semaphore_signal(near_sem, inc=1, device_id=sibling, device_id_type=MESH)

    def send(stage, src, dst, to):
        pltpu.make_async_remote_copy(
            src_ref=src,
            dst_ref=dst,
            send_sem=send_sem.at[stage],
            recv_sem=recv_sem.at[stage],
            device_id=to,
            device_id_type=MESH,
        ).start()

    def wait(sem, ref):
        pltpu.make_async_copy(ref, ref, sem).wait()

    row = lax.broadcasted_iota(jnp.int32, (REC, 128), 0)
    lane = lax.broadcasted_iota(jnp.int32, (REC, 128), 1)

    def chunk(value, j):
        return value[:, j * 128 : (j + 1) * 128]

    def core_major(rows):
        return jnp.concatenate([rows[2 * j + p : 2 * j + p + 1] for p in range(2) for j in range(8)], axis=0)

    loads[0].wait()
    logits = core_major(logits_v[0])
    raised_c = jnp.exp(logits - jnp.max(logits, axis=0, keepdims=True))
    combine = raised_c / jnp.sum(raised_c, axis=0, keepdims=True)
    peak = low(jnp.max(logits, axis=1, keepdims=True))
    raised = jnp.exp(logits - peak)
    total = jnp.sum(raised, axis=1, keepdims=True)
    loads[1].wait()
    gathered = dot(raised.astype(BF16), tokens_v[0], ((1,), (0,)))
    loads[2].wait()
    backs = dot(combine.astype(BF16), grads_v[0], ((1,), (0,)))
    for j in range(CH):
        sa[pl.ds(j, 16, stride=REC), :] = chunk(gathered, j)
        sa[pl.ds(CH + j, 16, stride=REC), :] = chunk(backs, j)
    sa[pl.ds(20, 16, stride=REC), :] = jnp.broadcast_to(peak, (16, 128))
    sa[pl.ds(21, 16, stride=REC), :] = jnp.broadcast_to(total, (16, 128))
    for i in (22, 23):
        sa[pl.ds(i, 16, stride=REC), :] = jnp.zeros((16, 128), F32)
    halves[pl.ds(PAIR, 8), :] = jnp.zeros((8, 128), F32)
    loads[3].wait()
    router = core_major(router_v[...].astype(F32))
    loads[4].wait()
    loads[5].wait()

    @pl.when(core == 1)
    def _():
        pl.semaphore_wait(near_sem, 1)

    send(0, sa.at[pl.ds((1 - core) * 192, 192)], ra, sibling)
    wait(recv_sem.at[0], ra)
    own = sa[pl.ds(pl.multiple_of(core * 192, 192), 192), :].reshape(8, REC, 128)
    other = ra[...].reshape(8, REC, 128)
    scaled = (row < CH) | (row == 21)
    top = jnp.maximum(own[:, 20:21, :], other[:, 20:21, :])
    both = own * jnp.where(scaled, jnp.exp(own[:, 20:21, :] - top), 1.0) + other * jnp.where(
        scaled, jnp.exp(other[:, 20:21, :] - top), 1.0
    )
    count = both[:, 21:22, :]
    both = jnp.where(row == 20, top, jnp.where(row == 22, count - low(count), both))
    sz[...] = both.astype(BF16)
    rz[pl.ds(z, 1)] = sz[pl.ds(zlo, 1)]

    @pl.when(core == 1)
    def _():
        pl.semaphore_wait(barrier, 60)
        pl.semaphore_signal(far_sem, inc=1, device_id=sibling, device_id_type=MESH)

    @pl.when(core == 0)
    def _():
        pl.semaphore_wait(far_sem, 1)

    for z_to in z_peers:
        send(1, sz.at[lax.rem(z_to, 8)], rz.at[z], device(z_to, xy, core))
    wait(recv_sem.at[1], rz.at[pl.ds(0, ZN - 1)])
    slots, tops, totals = [], [], []
    for h in range(2):
        part = rz[pl.ds(8 * h, 8)].astype(F32)
        peaks = part[:, 20:21, :]
        top = jnp.max(peaks, axis=0)
        factor = jnp.exp(peaks - top)
        count = jnp.sum(factor * (part[:, 21:22, :] + part[:, 22:23, :]), axis=0)
        summed = jnp.sum(part * jnp.where(row < CH, factor, 1.0), axis=0)
        slots.append(jnp.where(row < CH, summed / count, summed))
        tops.append(top)
        totals.append(count)
        sb[pl.ds(2 * CH * h, 2 * CH), :] = slots[h][: 2 * CH]
    packed = sb[...].astype(BF16)
    rb[pl.ds(xy, 1)] = packed[None]

    for xy_to in xy_peers:
        send(2, rb.at[xy], rb.at[xy], device(z, xy_to, core))
    wait(recv_sem.at[2], rb.at[pl.ds(0, XYN - 1)])
    wide[...] = rb[...].astype(F32).reshape(XYN * PAIR, 128)

    def clips(first):
        return jnp.concatenate(
            [
                jnp.concatenate(
                    [wide[pl.ds(h * 2 * CH + first + j, 16, stride=PAIR), :].astype(BF16) for j in range(CH)],
                    axis=1,
                )
                for h in range(2)
            ],
            axis=0,
        )

    every_in, every_back = clips(0), clips(CH)
    pre = dot(every_in, w_in_v[0], ((1,), (1,)))
    act_back = dot(every_back, w_out_v[0], ((1,), (1,)))
    slope = math.sqrt(2.0 / math.pi)
    bent = jnp.tanh(slope * (pre + 0.044715 * (pre * pre * pre)))
    activated = (0.5 * pre * (1.0 + bent)).astype(BF16)
    gelu_slope = 0.5 * (1.0 + bent) + 0.5 * pre * ((1.0 + bent) * (1.0 - bent)) * (
        slope * (1.0 + 3.0 * 0.044715 * (pre * pre))
    )
    hidden_back = (gelu_slope * act_back).astype(BF16)
    in_part = dot(hidden_back, w_in_v[0], ((1,), (0,)))
    out_part = dot(activated, w_out_v[0], ((1,), (0,)))
    for h in range(2):
        for j in range(CH):
            wide[pl.ds(h * 2 * CH + j, 16, stride=PAIR), :] = chunk(in_part, j)[16 * h : 16 * h + 16]
            wide[pl.ds(h * 2 * CH + CH + j, 16, stride=PAIR), :] = chunk(out_part, j)[16 * h : 16 * h + 16]
    sc[...] = wide[...].reshape(XYN, PAIR, 128).astype(BF16)
    rc[pl.ds(xy, 1)] = sc[pl.ds(xy, 1)]

    for xy_to in xy_peers:
        send(3, sc.at[xy_to], rc.at[xy], device(z, xy_to, core))
    w_out_grad_v[0] = dot(activated, every_back, ((0,), (0,))).astype(BF16)
    w_in_grad_v[0] = dot(hidden_back, every_in, ((0,), (0,))).astype(BF16)
    stores = [
        pltpu.make_async_copy(w_in_grad_v, w_in_grad_hbm, out_sem.at[0]),
        pltpu.make_async_copy(w_out_grad_v, w_out_grad_hbm, out_sem.at[1]),
        pltpu.make_async_copy(token_grad_v, token_grad_hbm, out_sem.at[2]),
    ]
    stores[0].start()
    stores[1].start()
    wait(recv_sem.at[3], rc.at[pl.ds(0, XYN - 1)])
    halves[pl.ds(0, PAIR), :] = jnp.sum(rc[...].astype(F32), axis=0)
    for h in range(2):
        half = halves[pl.ds(2 * CH * h, REC), :]
        dotted = jnp.sum(jnp.where(row < CH, low(half) * slots[h], 0.0), keepdims=True)
        half = jnp.where(row == 20, tops[h], half)
        half = jnp.where(row == 21, totals[h], half)
        half = jnp.where(row == 22, totals[h] - low(totals[h]), half)
        half = jnp.where(row == 23, jnp.where(lane < 64, dotted, dotted - low(dotted)), half)
        sd[pl.ds(h, 1)] = half.astype(BF16)[None]
    rd[pl.ds(z, 1)] = sd[pl.ds(zhi, 1)]

    for z_to in z_peers:
        send(4, sd.at[z_to // 8], rd.at[z], device(z_to, xy, core))
    wait(recv_sem.at[4], rd.at[pl.ds(0, ZN - 1)])
    first, second = rd[pl.ds(0, 8)].astype(F32), rd[pl.ds(8, 8)].astype(F32)
    both = first + second
    dotted = both[:, 23:24, 0:1] + both[:, 23:24, 64:65]
    both = jnp.where(row == 20, first, both)
    both = jnp.where(row == 21, first[:, 21:22, :] + first[:, 22:23, :], both)
    both = jnp.where(row == 23, dotted, both)
    mine = pl.ds(pl.multiple_of(core * 192, 192), 192)
    se[mine, :] = both.reshape(192, 128)

    send(5, se.at[mine], se.at[mine], sibling)
    wait(recv_sem.at[5], ra)

    def slot_rows(first):
        return jnp.concatenate([se[pl.ds(first + j, 16, stride=REC), :] for j in range(CH)], axis=1).astype(BF16)

    in_back, slot_out = slot_rows(0), slot_rows(CH)
    col_peak = se[pl.ds(20, 16, stride=REC), :][:, 0:1]
    col_total = se[pl.ds(21, 16, stride=REC), :][:, 0:1]
    slot_total = se[pl.ds(23, 16, stride=REC), :][:, 0:1]
    dispatch = (jnp.exp(logits - col_peak) / col_total).astype(BF16)
    weights = dispatch.astype(F32)
    combine_back = dot(slot_out, grads_v[0], ((1,), (1,)))
    dispatch_back = dot(in_back, tokens_v[0], ((1,), (1,)))
    logit_comb = combine * (combine_back - jnp.sum(combine * combine_back, axis=0, keepdims=True))
    logit_back = (logit_comb + weights * (dispatch_back - slot_total)).astype(BF16)
    router_part = dot(logit_back, tokens_v[0], ((1,), (0,)))
    for j in range(CH):
        rows[pl.ds(j, 16, stride=16), :] = chunk(router_part, j)
    for j in range(CH, 16):
        rows[pl.ds(j, 16, stride=16), :] = jnp.zeros((16, 128), F32)
    sf[...] = rows[...].reshape(16, 16, 128).astype(BF16)
    rf[pl.ds(xy, 1)] = sf[pl.ds(xy, 1)]

    for xy_to in xy_peers:
        send(6, sf.at[xy_to], rf.at[xy], device(z, xy_to, core))
    left = jnp.concatenate([weights, logit_back.astype(F32)], axis=0).astype(BF16)
    right = jnp.concatenate([in_back.astype(F32), router], axis=0).astype(BF16)
    token_grad_v[0] = (dot(left, right, ((0,), (0,))) * 64.0).astype(BF16)
    stores[2].start()
    wait(recv_sem.at[6], rf.at[pl.ds(0, XYN - 1)])
    own_row[...] = jnp.sum(rf[...].astype(F32), axis=0)
    send(9, own_row, other_row, sibling)
    wait(recv_sem.at[9], other_row)
    sh[...] = (own_row[...] + other_row[...]).astype(BF16)
    rh[pl.ds(z, 1)] = sh[...][None]

    for z_to in z_peers:
        send(7, sh, rh.at[z], device(z_to, xy, core))
    wait(recv_sem.at[7], rh.at[pl.ds(0, ZN - 1)])
    place = lax.rem(xy, 8) * 2 + xy // 8
    summed_row[...] = jnp.sum(rh[...].astype(F32), axis=0, keepdims=True).astype(BF16)

    for xy_to in xy_peers:
        send(8, summed_row.at[0], ri.at[place], device(z, xy_to, core))
    kept = pltpu.make_async_copy(summed_row.at[0], ri.at[place], out_sem.at[3])
    kept.start()
    stores.append(kept)
    wait(recv_sem.at[8], ri.at[pl.ds(0, 15)])

    wait(send_sem.at[0], ra)
    wait(send_sem.at[1], rz.at[pl.ds(0, ZN - 1)])
    wait(send_sem.at[2], rb.at[pl.ds(0, XYN - 1)])
    wait(send_sem.at[3], rc.at[pl.ds(0, XYN - 1)])
    wait(send_sem.at[4], rd.at[pl.ds(0, ZN - 1)])
    wait(send_sem.at[5], ra)
    wait(send_sem.at[6], rf.at[pl.ds(0, XYN - 1)])
    wait(send_sem.at[7], rh.at[pl.ds(0, ZN - 1)])
    wait(send_sem.at[8], ri.at[pl.ds(0, 15)])
    wait(send_sem.at[9], other_row)
    for copy in stores:
        copy.wait()


def store_kernel(
    token_grad, ri, w_in_grad, w_out_grad,
    token_grad_hbm, router_grad_hbm, w_in_grad_hbm, w_out_grad_hbm,
    ri_v, rows, router_grad_v, sems,
):
    gather = pltpu.make_async_copy(ri, ri_v, sems.at[0])
    gather.start()
    copies = [
        pltpu.make_async_copy(token_grad, token_grad_hbm, sems.at[1]),
        pltpu.make_async_copy(w_in_grad, w_in_grad_hbm, sems.at[2]),
        pltpu.make_async_copy(w_out_grad, w_out_grad_hbm, sems.at[3]),
        pltpu.make_async_copy(router_grad_v, router_grad_hbm, sems.at[4]),
    ]
    for copy in copies[:3]:
        copy.start()
    gather.wait()
    rows[...] = (ri_v[...].astype(F32) / math.sqrt(32.0)).reshape(256, 128)
    for j in range(CH):
        router_grad_v[:, j * 128 : (j + 1) * 128] = rows[pl.ds(j, 16, stride=16), :]
    copies[3].start()
    for copy in copies:
        copy.wait()


def local(tokens, out_grad, logits, router, w_in, w_out):
    anywhere = pl.BlockSpec(memory_space=pl.ANY)
    hbm = pl.BlockSpec(memory_space=pltpu.HBM)
    w_in = jnp.swapaxes(w_in, 1, 2)
    inputs = tuple(
        pltpu.with_memory_space_constraint(a, pltpu.HBM) for a in (tokens, out_grad, logits, router, w_in, w_out)
    )
    results = (
        jax.ShapeDtypeStruct(tokens.shape, BF16),
        jax.ShapeDtypeStruct(router.shape, F32),
        jax.ShapeDtypeStruct(w_in.shape, BF16),
        jax.ShapeDtypeStruct(w_out.shape, BF16),
    )
    made = pl.pallas_call(
        kernel,
        name="moe_back",
        out_shape=tuple(
            pltpu.VMEM(shape, BF16) for shape in (tokens.shape, (16, 16, 128), w_in.shape, w_out.shape)
        ),
        in_specs=[hbm] * 6,
        out_specs=(anywhere,) * 4,
        scratch_shapes=[pltpu.VMEM(a.shape, a.dtype) for a in inputs]
        + [
            pltpu.VMEM(tokens.shape, BF16),
            pltpu.VMEM(w_in.shape, BF16),
            pltpu.VMEM(w_out.shape, BF16),
            pltpu.VMEM((16 * REC, 128), F32),
            pltpu.VMEM((8 * REC, 128), F32),
            pltpu.VMEM((8, REC, 128), BF16),
            pltpu.VMEM((ZN, REC, 128), BF16),
            pltpu.VMEM((PAIR, 128), F32),
            pltpu.VMEM((XYN, PAIR, 128), BF16),
            pltpu.VMEM((XYN * PAIR, 128), F32),
            pltpu.VMEM((XYN, PAIR, 128), BF16),
            pltpu.VMEM((XYN, PAIR, 128), BF16),
            pltpu.VMEM((48, 128), F32),
            pltpu.VMEM((2, REC, 128), BF16),
            pltpu.VMEM((ZN, REC, 128), BF16),
            pltpu.VMEM((16 * REC, 128), F32),
            pltpu.VMEM((16 * 16, 128), F32),
            pltpu.VMEM((16, 16, 128), BF16),
            pltpu.VMEM((XYN, 16, 128), BF16),
            pltpu.VMEM((16, 128), F32),
            pltpu.VMEM((16, 128), F32),
            pltpu.VMEM((16, 128), BF16),
            pltpu.VMEM((ZN, 16, 128), BF16),
            pltpu.VMEM((1, 16, 128), BF16),
            pltpu.SemaphoreType.DMA((6,)),
            pltpu.SemaphoreType.DMA((4,)),
            pltpu.SemaphoreType.DMA((10,)),
            pltpu.SemaphoreType.DMA((10,)),
            pltpu.SemaphoreType.REGULAR,
            pltpu.SemaphoreType.REGULAR,
        ],
        compiler_params=pltpu.CompilerParams(
            collective_id=0, has_side_effects=True, vmem_limit_bytes=32 * 1024 * 1024
        ),
    )(*inputs)
    token_grad, router_grad, w_in_grad, w_out_grad = pl.pallas_call(
        store_kernel,
        name="store",
        out_shape=results,
        in_specs=[anywhere] * 4,
        out_specs=(hbm,) * 4,
        scratch_shapes=[
            pltpu.VMEM((16, 16, 128), BF16),
            pltpu.VMEM((256, 128), F32),
            pltpu.VMEM(router.shape, F32),
            pltpu.SemaphoreType.DMA((5,)),
        ],
    )(*(pltpu.with_memory_space_constraint(a, pltpu.VMEM) for a in made))
    return (token_grad, router_grad, jnp.swapaxes(w_in_grad, 1, 2), w_out_grad)


def solution(mesh):
    return jax.shard_map(
        local,
        mesh=mesh,
        in_specs=(
            P("dp", "seq", None),
            P("dp", "seq", None),
            P("dp", None, "seq"),
            P(),
            P("seq", None, "dp"),
            P("seq", "dp", None),
        ),
        out_specs=(P("dp", "seq", None), P(), P("seq", None, "dp"), P("seq", "dp", None)),
        check_vma=False,
    )
```

```python
import functools
import math

import jax
import jax.numpy as jnp
from jax import lax
from jax.experimental import pallas as pl
from jax.experimental.pallas import tpu as pltpu
from jax.sharding import PartitionSpec as P

MESH = pl.DeviceIdType.MESH
F32 = jnp.float32
BF16 = jnp.bfloat16

D = 1280
CH = D // 128
PAIR = 4 * CH
REC = 24
ZN = 16
XYN = 16
Z_ORDER = (8, 9, 7, 10, 6, 11, 5, 12, 4, 13, 3, 14, 2, 15, 1)
XY_ORDER = (
    (2, 2), (2, 1), (2, 3), (1, 2), (3, 2), (1, 1), (1, 3), (3, 1), (3, 3), (2, 0), (0, 2), (1, 0), (3, 0), (0, 1), (0, 3),
)


def low(value):
    return value.astype(BF16).astype(F32)


def dot(left, right, dims):
    return lax.dot_general(left, right, (dims, ((), ())), preferred_element_type=F32)


def kernel(
    tokens_hbm, grads_hbm, logits_hbm, router_hbm, w_in_hbm, w_out_hbm,
    token_grad_hbm, ri, w_in_grad_hbm, w_out_grad_hbm,
    tokens_v, grads_v, logits_v, router_v, w_in_v, w_out_v, token_grad_v, w_in_grad_v, w_out_grad_v,
    sa, ra, sz, rz, sb, rb, wide, sc, rc, halves, sd, rd, se, rows, sf, rf, own_row, other_row, sh, rh, summed_row,
    in_sem, out_sem, send_sem, recv_sem, near_sem, far_sem,
):
    dp, sq = lax.axis_index("dp"), lax.axis_index("seq")
    zhi, xy = dp // 16, lax.rem(dp, 16)
    zlo, core = sq // 2, lax.rem(sq, 2)
    z = zhi * 8 + zlo
    x, y = xy // 4, lax.rem(xy, 4)

    def device(z_to, xy_to, core_to):
        return (z_to // 8 * 16 + xy_to, lax.rem(z_to, 8) * 2 + core_to)

    z_peers = [lax.rem(z + k, ZN) for k in Z_ORDER]
    xy_peers = [lax.rem(x + dx, 4) * 4 + lax.rem(y + dy, 4) for dx, dy in XY_ORDER]
    sibling = device(z, xy, 1 - core)

    barrier = pltpu.get_barrier_semaphore()

    @pl.when(core == 1)
    def _():
        pl.semaphore_signal(barrier, inc=1, device_id=sibling, device_id_type=MESH)

    for z_to in z_peers:
        pl.semaphore_signal(barrier, inc=1, device_id=device(z_to, xy, 1), device_id_type=MESH)
    for xy_to in xy_peers:
        pl.semaphore_signal(barrier, inc=1, device_id=device(z, xy_to, 1), device_id_type=MESH)

    loads = []
    for i, (src, dst) in enumerate(
        (
            (logits_hbm, logits_v),
            (tokens_hbm, tokens_v),
            (grads_hbm, grads_v),
            (router_hbm, router_v),
            (w_in_hbm, w_in_v),
            (w_out_hbm, w_out_v),
        )
    ):
        copy = pltpu.make_async_copy(src, dst, in_sem.at[i])
        copy.start()
        loads.append(copy)

    def send(stage, src, dst, to):
        pltpu.make_async_remote_copy(
            src_ref=src,
            dst_ref=dst,
            send_sem=send_sem.at[stage],
            recv_sem=recv_sem.at[stage],
            device_id=to,
            device_id_type=MESH,
        ).start()

    def wait(sem, ref):
        pltpu.make_async_copy(ref, ref, sem).wait()

    row = lax.broadcasted_iota(jnp.int32, (REC, 128), 0)
    lane = lax.broadcasted_iota(jnp.int32, (REC, 128), 1)

    def chunk(value, j):
        return value[:, j * 128 : (j + 1) * 128]

    def core_major(rows):
        return jnp.concatenate([rows[2 * j + p : 2 * j + p + 1] for p in range(2) for j in range(8)], axis=0)

    loads[0].wait()
    logits = core_major(logits_v[0])
    raised_c = jnp.exp(logits - jnp.max(logits, axis=0, keepdims=True))
    combine = raised_c / jnp.sum(raised_c, axis=0, keepdims=True)
    peak = low(jnp.max(logits, axis=1, keepdims=True))
    raised = jnp.exp(logits - peak)
    total = jnp.sum(raised, axis=1, keepdims=True)
    loads[1].wait()
    gathered = dot(raised.astype(BF16), tokens_v[0], ((1,), (0,)))
    loads[2].wait()
    backs = dot(combine.astype(BF16), grads_v[0], ((1,), (0,)))
    for j in range(CH):
        sa[pl.ds(j, 16, stride=REC), :] = chunk(gathered, j)
        sa[pl.ds(CH + j, 16, stride=REC), :] = chunk(backs, j)
    sa[pl.ds(20, 16, stride=REC), :] = jnp.broadcast_to(peak, (16, 128))
    sa[pl.ds(21, 16, stride=REC), :] = jnp.broadcast_to(total, (16, 128))
    for i in (22, 23):
        sa[pl.ds(i, 16, stride=REC), :] = jnp.zeros((16, 128), F32)
    halves[pl.ds(PAIR, 8), :] = jnp.zeros((8, 128), F32)
    loads[3].wait()
    router = core_major(router_v[...].astype(F32))
    loads[4].wait()
    loads[5].wait()

    @pl.when(core == 0)
    def _():
        pl.semaphore_wait(barrier, 1)
        pl.semaphore_signal(near_sem, inc=1, device_id=sibling, device_id_type=MESH)

    @pl.when(core == 1)
    def _():
        pl.semaphore_wait(near_sem, 1)

    send(0, sa.at[pl.ds((1 - core) * 192, 192)], ra, sibling)
    wait(recv_sem.at[0], ra)
    own = sa[pl.ds(pl.multiple_of(core * 192, 192), 192), :].reshape(8, REC, 128)
    other = ra[...].reshape(8, REC, 128)
    scaled = (row < CH) | (row == 21)
    top = jnp.maximum(own[:, 20:21, :], other[:, 20:21, :])
    both = own * jnp.where(scaled, jnp.exp(own[:, 20:21, :] - top), 1.0) + other * jnp.where(
        scaled, jnp.exp(other[:, 20:21, :] - top), 1.0
    )
    count = both[:, 21:22, :]
    both = jnp.where(row == 20, top, jnp.where(row == 22, count - low(count), both))
    sz[...] = both.astype(BF16)
    rz[pl.ds(z, 1)] = sz[pl.ds(zlo, 1)]

    @pl.when(core == 1)
    def _():
        pl.semaphore_wait(barrier, 60)
        pl.semaphore_signal(far_sem, inc=1, device_id=sibling, device_id_type=MESH)

    @pl.when(core == 0)
    def _():
        pl.semaphore_wait(far_sem, 1)

    for z_to in z_peers:
        send(1, sz.at[lax.rem(z_to, 8)], rz.at[z], device(z_to, xy, core))
    wait(recv_sem.at[1], rz.at[pl.ds(0, ZN - 1)])
    slots, tops, totals = [], [], []
    for h in range(2):
        part = rz[pl.ds(8 * h, 8)].astype(F32)
        peaks = part[:, 20:21, :]
        top = jnp.max(peaks, axis=0)
        factor = jnp.exp(peaks - top)
        count = jnp.sum(factor * (part[:, 21:22, :] + part[:, 22:23, :]), axis=0)
        summed = jnp.sum(part * jnp.where(row < CH, factor, 1.0), axis=0)
        slots.append(jnp.where(row < CH, summed / count, summed))
        tops.append(top)
        totals.append(count)
        sb[pl.ds(2 * CH * h, 2 * CH), :] = slots[h][: 2 * CH]
    packed = sb[...].astype(BF16)
    rb[pl.ds(xy, 1)] = packed[None]

    for xy_to in xy_peers:
        send(2, rb.at[xy], rb.at[xy], device(z, xy_to, core))
    wait(recv_sem.at[2], rb.at[pl.ds(0, XYN - 1)])
    wide[...] = rb[...].astype(F32).reshape(XYN * PAIR, 128)

    def clips(first):
        return jnp.concatenate(
            [
                jnp.concatenate(
                    [wide[pl.ds(h * 2 * CH + first + j, 16, stride=PAIR), :].astype(BF16) for j in range(CH)],
                    axis=1,
                )
                for h in range(2)
            ],
            axis=0,
        )

    every_in, every_back = clips(0), clips(CH)
    pre = dot(every_in, w_in_v[0], ((1,), (1,)))
    act_back = dot(every_back, w_out_v[0], ((1,), (1,)))
    slope = math.sqrt(2.0 / math.pi)
    bent = jnp.tanh(slope * (pre + 0.044715 * (pre * pre * pre)))
    activated = (0.5 * pre * (1.0 + bent)).astype(BF16)
    gelu_slope = 0.5 * (1.0 + bent) + 0.5 * pre * ((1.0 + bent) * (1.0 - bent)) * (
        slope * (1.0 + 3.0 * 0.044715 * (pre * pre))
    )
    hidden_back = (gelu_slope * act_back).astype(BF16)
    in_part = dot(hidden_back, w_in_v[0], ((1,), (0,)))
    out_part = dot(activated, w_out_v[0], ((1,), (0,)))
    for h in range(2):
        for j in range(CH):
            wide[pl.ds(h * 2 * CH + j, 16, stride=PAIR), :] = chunk(in_part, j)[16 * h : 16 * h + 16]
            wide[pl.ds(h * 2 * CH + CH + j, 16, stride=PAIR), :] = chunk(out_part, j)[16 * h : 16 * h + 16]
    sc[...] = wide[...].reshape(XYN, PAIR, 128).astype(BF16)
    rc[pl.ds(xy, 1)] = sc[pl.ds(xy, 1)]

    for xy_to in xy_peers:
        send(3, sc.at[xy_to], rc.at[xy], device(z, xy_to, core))
    w_out_grad_v[0] = dot(activated, every_back, ((0,), (0,))).astype(BF16)
    w_in_grad_v[0] = dot(hidden_back, every_in, ((0,), (0,))).astype(BF16)
    stores = [
        pltpu.make_async_copy(w_in_grad_v, w_in_grad_hbm, out_sem.at[0]),
        pltpu.make_async_copy(w_out_grad_v, w_out_grad_hbm, out_sem.at[1]),
        pltpu.make_async_copy(token_grad_v, token_grad_hbm, out_sem.at[2]),
    ]
    stores[0].start()
    stores[1].start()
    wait(recv_sem.at[3], rc.at[pl.ds(0, XYN - 1)])
    halves[pl.ds(0, PAIR), :] = jnp.sum(rc[...].astype(F32), axis=0)
    for h in range(2):
        half = halves[pl.ds(2 * CH * h, REC), :]
        dotted = jnp.sum(jnp.where(row < CH, low(half) * slots[h], 0.0), keepdims=True)
        half = jnp.where(row == 20, tops[h], half)
        half = jnp.where(row == 21, totals[h], half)
        half = jnp.where(row == 22, totals[h] - low(totals[h]), half)
        half = jnp.where(row == 23, jnp.where(lane < 64, dotted, dotted - low(dotted)), half)
        sd[pl.ds(h, 1)] = half.astype(BF16)[None]
    rd[pl.ds(z, 1)] = sd[pl.ds(zhi, 1)]

    for z_to in z_peers:
        send(4, sd.at[z_to // 8], rd.at[z], device(z_to, xy, core))
    wait(recv_sem.at[4], rd.at[pl.ds(0, ZN - 1)])
    first, second = rd[pl.ds(0, 8)].astype(F32), rd[pl.ds(8, 8)].astype(F32)
    both = first + second
    dotted = both[:, 23:24, 0:1] + both[:, 23:24, 64:65]
    both = jnp.where(row == 20, first, both)
    both = jnp.where(row == 21, first[:, 21:22, :] + first[:, 22:23, :], both)
    both = jnp.where(row == 23, dotted, both)
    mine = pl.ds(pl.multiple_of(core * 192, 192), 192)
    se[mine, :] = both.reshape(192, 128)

    send(5, se.at[mine], se.at[mine], sibling)
    wait(recv_sem.at[5], ra)

    def slot_rows(first):
        return jnp.concatenate([se[pl.ds(first + j, 16, stride=REC), :] for j in range(CH)], axis=1).astype(BF16)

    in_back, slot_out = slot_rows(0), slot_rows(CH)
    col_peak = se[pl.ds(20, 16, stride=REC), :][:, 0:1]
    col_total = se[pl.ds(21, 16, stride=REC), :][:, 0:1]
    slot_total = se[pl.ds(23, 16, stride=REC), :][:, 0:1]
    dispatch = (jnp.exp(logits - col_peak) / col_total).astype(BF16)
    weights = dispatch.astype(F32)
    combine_back = dot(slot_out, grads_v[0], ((1,), (1,)))
    dispatch_back = dot(in_back, tokens_v[0], ((1,), (1,)))
    logit_comb = combine * (combine_back - jnp.sum(combine * combine_back, axis=0, keepdims=True))
    logit_back = (logit_comb + weights * (dispatch_back - slot_total)).astype(BF16)
    router_part = dot(logit_back, tokens_v[0], ((1,), (0,)))
    for j in range(CH):
        rows[pl.ds(j, 16, stride=16), :] = chunk(router_part, j)
    for j in range(CH, 16):
        rows[pl.ds(j, 16, stride=16), :] = jnp.zeros((16, 128), F32)
    sf[...] = rows[...].reshape(16, 16, 128).astype(BF16)
    rf[pl.ds(xy, 1)] = sf[pl.ds(xy, 1)]

    for xy_to in xy_peers:
        send(6, sf.at[xy_to], rf.at[xy], device(z, xy_to, core))
    left = jnp.concatenate([weights, logit_back.astype(F32)], axis=0).astype(BF16)
    right = jnp.concatenate([in_back.astype(F32), router], axis=0).astype(BF16)
    token_grad_v[0] = (dot(left, right, ((0,), (0,))) * 64.0).astype(BF16)
    stores[2].start()
    wait(recv_sem.at[6], rf.at[pl.ds(0, XYN - 1)])
    own_row[...] = jnp.sum(rf[...].astype(F32), axis=0)
    send(9, own_row, other_row, sibling)
    wait(recv_sem.at[9], other_row)
    sh[...] = (own_row[...] + other_row[...]).astype(BF16)
    rh[pl.ds(z, 1)] = sh[...][None]

    for z_to in z_peers:
        send(7, sh, rh.at[z], device(z_to, xy, core))
    wait(recv_sem.at[7], rh.at[pl.ds(0, ZN - 1)])
    place = lax.rem(xy, 8) * 2 + xy // 8
    summed_row[...] = jnp.sum(rh[...].astype(F32), axis=0, keepdims=True).astype(BF16)

    for xy_to in xy_peers:
        send(8, summed_row.at[0], ri.at[place], device(z, xy_to, core))
    kept = pltpu.make_async_copy(summed_row.at[0], ri.at[place], out_sem.at[3])
    kept.start()
    stores.append(kept)
    wait(recv_sem.at[8], ri.at[pl.ds(0, 15)])

    wait(send_sem.at[0], ra)
    wait(send_sem.at[1], rz.at[pl.ds(0, ZN - 1)])
    wait(send_sem.at[2], rb.at[pl.ds(0, XYN - 1)])
    wait(send_sem.at[3], rc.at[pl.ds(0, XYN - 1)])
    wait(send_sem.at[4], rd.at[pl.ds(0, ZN - 1)])
    wait(send_sem.at[5], ra)
    wait(send_sem.at[6], rf.at[pl.ds(0, XYN - 1)])
    wait(send_sem.at[7], rh.at[pl.ds(0, ZN - 1)])
    wait(send_sem.at[8], ri.at[pl.ds(0, 15)])
    wait(send_sem.at[9], other_row)
    for copy in stores:
        copy.wait()


def store_kernel(
    token_grad, ri, w_in_grad, w_out_grad,
    token_grad_hbm, router_grad_hbm, w_in_grad_hbm, w_out_grad_hbm,
    ri_v, rows, router_grad_v, sems,
):
    gather = pltpu.make_async_copy(ri, ri_v, sems.at[0])
    gather.start()
    copies = [
        pltpu.make_async_copy(token_grad, token_grad_hbm, sems.at[1]),
        pltpu.make_async_copy(w_in_grad, w_in_grad_hbm, sems.at[2]),
        pltpu.make_async_copy(w_out_grad, w_out_grad_hbm, sems.at[3]),
        pltpu.make_async_copy(router_grad_v, router_grad_hbm, sems.at[4]),
    ]
    for copy in copies[:3]:
        copy.start()
    gather.wait()
    rows[...] = (ri_v[...].astype(F32) / math.sqrt(32.0)).reshape(256, 128)
    for j in range(CH):
        router_grad_v[:, j * 128 : (j + 1) * 128] = rows[pl.ds(j, 16, stride=16), :]
    copies[3].start()
    for copy in copies:
        copy.wait()


def local(tokens, out_grad, logits, router, w_in, w_out):
    anywhere = pl.BlockSpec(memory_space=pl.ANY)
    hbm = pl.BlockSpec(memory_space=pltpu.HBM)
    w_in = jnp.swapaxes(w_in, 1, 2)
    inputs = tuple(
        pltpu.with_memory_space_constraint(a, pltpu.HBM) for a in (tokens, out_grad, logits, router, w_in, w_out)
    )
    results = (
        jax.ShapeDtypeStruct(tokens.shape, BF16),
        jax.ShapeDtypeStruct(router.shape, F32),
        jax.ShapeDtypeStruct(w_in.shape, BF16),
        jax.ShapeDtypeStruct(w_out.shape, BF16),
    )
    made = pl.pallas_call(
        kernel,
        name="moe_back",
        out_shape=tuple(
            pltpu.VMEM(shape, BF16) for shape in (tokens.shape, (16, 16, 128), w_in.shape, w_out.shape)
        ),
        in_specs=[hbm] * 6,
        out_specs=(anywhere,) * 4,
        scratch_shapes=[pltpu.VMEM(a.shape, a.dtype) for a in inputs]
        + [
            pltpu.VMEM(tokens.shape, BF16),
            pltpu.VMEM(w_in.shape, BF16),
            pltpu.VMEM(w_out.shape, BF16),
            pltpu.VMEM((16 * REC, 128), F32),
            pltpu.VMEM((8 * REC, 128), F32),
            pltpu.VMEM((8, REC, 128), BF16),
            pltpu.VMEM((ZN, REC, 128), BF16),
            pltpu.VMEM((PAIR, 128), F32),
            pltpu.VMEM((XYN, PAIR, 128), BF16),
            pltpu.VMEM((XYN * PAIR, 128), F32),
            pltpu.VMEM((XYN, PAIR, 128), BF16),
            pltpu.VMEM((XYN, PAIR, 128), BF16),
            pltpu.VMEM((48, 128), F32),
            pltpu.VMEM((2, REC, 128), BF16),
            pltpu.VMEM((ZN, REC, 128), BF16),
            pltpu.VMEM((16 * REC, 128), F32),
            pltpu.VMEM((16 * 16, 128), F32),
            pltpu.VMEM((16, 16, 128), BF16),
            pltpu.VMEM((XYN, 16, 128), BF16),
            pltpu.VMEM((16, 128), F32),
            pltpu.VMEM((16, 128), F32),
            pltpu.VMEM((16, 128), BF16),
            pltpu.VMEM((ZN, 16, 128), BF16),
            pltpu.VMEM((1, 16, 128), BF16),
            pltpu.SemaphoreType.DMA((6,)),
            pltpu.SemaphoreType.DMA((4,)),
            pltpu.SemaphoreType.DMA((10,)),
            pltpu.SemaphoreType.DMA((10,)),
            pltpu.SemaphoreType.REGULAR,
            pltpu.SemaphoreType.REGULAR,
        ],
        compiler_params=pltpu.CompilerParams(
            collective_id=0, has_side_effects=True, vmem_limit_bytes=32 * 1024 * 1024
        ),
    )(*inputs)
    token_grad, router_grad, w_in_grad, w_out_grad = pl.pallas_call(
        store_kernel,
        name="store",
        out_shape=results,
        in_specs=[anywhere] * 4,
        out_specs=(hbm,) * 4,
        scratch_shapes=[
            pltpu.VMEM((16, 16, 128), BF16),
            pltpu.VMEM((256, 128), F32),
            pltpu.VMEM(router.shape, F32),
            pltpu.SemaphoreType.DMA((5,)),
        ],
    )(*(pltpu.with_memory_space_constraint(a, pltpu.VMEM) for a in made))
    return (token_grad, router_grad, jnp.swapaxes(w_in_grad, 1, 2), w_out_grad)


def solution(mesh):
    return jax.shard_map(
        local,
        mesh=mesh,
        in_specs=(
            P("dp", "seq", None),
            P("dp", "seq", None),
            P("dp", None, "seq"),
            P(),
            P("seq", None, "dp"),
            P("seq", "dp", None),
        ),
        out_specs=(P("dp", "seq", None), P(), P("seq", None, "dp"), P("seq", "dp", None)),
        check_vma=False,
    )
```

```python
import functools
import math

import jax
import jax.numpy as jnp
from jax import lax
from jax.experimental import pallas as pl
from jax.experimental.pallas import tpu as pltpu
from jax.sharding import PartitionSpec as P

MESH = pl.DeviceIdType.MESH
F32 = jnp.float32
BF16 = jnp.bfloat16

D = 1280
CH = D // 128
PAIR = 4 * CH
REC = 24
ZN = 16
XYN = 16
Z_ORDER = (8, 9, 7, 10, 6, 11, 5, 12, 4, 13, 3, 14, 2, 15, 1)
XY_ORDER = (
    (2, 2), (2, 1), (2, 3), (1, 2), (3, 2), (1, 1), (1, 3), (3, 1), (3, 3), (2, 0), (0, 2), (1, 0), (3, 0), (0, 1), (0, 3),
)


def low(value):
    return value.astype(BF16).astype(F32)


def dot(left, right, dims):
    return lax.dot_general(left, right, (dims, ((), ())), preferred_element_type=F32)


def kernel(
    tokens_hbm, grads_hbm, logits_hbm, router_hbm, w_in_hbm, w_out_hbm,
    token_grad_v, ri, w_in_grad_v, w_out_grad_v,
    tokens_v, grads_v, logits_v, router_v, w_in_v, w_out_v,
    sa, ra, sz, rz, sb, rb, wide, sc, rc, halves, sd, rd, se, rows, sf, rf, own_row, other_row, sh, rh, summed_row,
    in_sem, out_sem, send_sem, recv_sem, near_sem, far_sem,
):
    dp, sq = lax.axis_index("dp"), lax.axis_index("seq")
    zhi, xy = dp // 16, lax.rem(dp, 16)
    zlo, core = sq // 2, lax.rem(sq, 2)
    z = zhi * 8 + zlo
    x, y = xy // 4, lax.rem(xy, 4)

    def device(z_to, xy_to, core_to):
        return (z_to // 8 * 16 + xy_to, lax.rem(z_to, 8) * 2 + core_to)

    z_peers = [lax.rem(z + k, ZN) for k in Z_ORDER]
    xy_peers = [lax.rem(x + dx, 4) * 4 + lax.rem(y + dy, 4) for dx, dy in XY_ORDER]
    sibling = device(z, xy, 1 - core)

    barrier = pltpu.get_barrier_semaphore()

    @pl.when(core == 1)
    def _():
        pl.semaphore_signal(barrier, inc=1, device_id=sibling, device_id_type=MESH)

    for z_to in z_peers:
        pl.semaphore_signal(barrier, inc=1, device_id=device(z_to, xy, 1), device_id_type=MESH)
    for xy_to in xy_peers:
        pl.semaphore_signal(barrier, inc=1, device_id=device(z, xy_to, 1), device_id_type=MESH)

    loads = []
    for i, (src, dst) in enumerate(
        (
            (logits_hbm, logits_v),
            (tokens_hbm, tokens_v),
            (grads_hbm, grads_v),
            (router_hbm, router_v),
            (w_in_hbm, w_in_v),
            (w_out_hbm, w_out_v),
        )
    ):
        copy = pltpu.make_async_copy(src, dst, in_sem.at[i])
        copy.start()
        loads.append(copy)

    def send(stage, src, dst, to):
        pltpu.make_async_remote_copy(
            src_ref=src,
            dst_ref=dst,
            send_sem=send_sem.at[stage],
            recv_sem=recv_sem.at[stage],
            device_id=to,
            device_id_type=MESH,
        ).start()

    def wait(sem, ref):
        pltpu.make_async_copy(ref, ref, sem).wait()

    row = lax.broadcasted_iota(jnp.int32, (REC, 128), 0)
    lane = lax.broadcasted_iota(jnp.int32, (REC, 128), 1)

    def chunk(value, j):
        return value[:, j * 128 : (j + 1) * 128]

    def core_major(rows):
        return jnp.concatenate([rows[2 * j + p : 2 * j + p + 1] for p in range(2) for j in range(8)], axis=0)

    loads[0].wait()
    logits = core_major(logits_v[0])
    raised_c = jnp.exp(logits - jnp.max(logits, axis=0, keepdims=True))
    combine = raised_c / jnp.sum(raised_c, axis=0, keepdims=True)
    peak = low(jnp.max(logits, axis=1, keepdims=True))
    raised = jnp.exp(logits - peak)
    total = jnp.sum(raised, axis=1, keepdims=True)
    loads[1].wait()
    gathered = dot(raised.astype(BF16), tokens_v[0], ((1,), (0,)))
    loads[2].wait()
    backs = dot(combine.astype(BF16), grads_v[0], ((1,), (0,)))
    for j in range(CH):
        sa[pl.ds(j, 16, stride=REC), :] = chunk(gathered, j)
        sa[pl.ds(CH + j, 16, stride=REC), :] = chunk(backs, j)
    sa[pl.ds(20, 16, stride=REC), :] = jnp.broadcast_to(peak, (16, 128))
    sa[pl.ds(21, 16, stride=REC), :] = jnp.broadcast_to(total, (16, 128))
    for i in (22, 23):
        sa[pl.ds(i, 16, stride=REC), :] = jnp.zeros((16, 128), F32)
    halves[pl.ds(PAIR, 8), :] = jnp.zeros((8, 128), F32)
    loads[3].wait()
    router = core_major(router_v[...].astype(F32))
    loads[4].wait()
    loads[5].wait()

    @pl.when(core == 0)
    def _():
        pl.semaphore_wait(barrier, 1)
        pl.semaphore_signal(near_sem, inc=1, device_id=sibling, device_id_type=MESH)

    @pl.when(core == 1)
    def _():
        pl.semaphore_wait(near_sem, 1)

    send(0, sa.at[pl.ds((1 - core) * 192, 192)], ra, sibling)
    wait(recv_sem.at[0], ra)
    own = sa[pl.ds(pl.multiple_of(core * 192, 192), 192), :].reshape(8, REC, 128)
    other = ra[...].reshape(8, REC, 128)
    scaled = (row < CH) | (row == 21)
    top = jnp.maximum(own[:, 20:21, :], other[:, 20:21, :])
    both = own * jnp.where(scaled, jnp.exp(own[:, 20:21, :] - top), 1.0) + other * jnp.where(
        scaled, jnp.exp(other[:, 20:21, :] - top), 1.0
    )
    count = both[:, 21:22, :]
    both = jnp.where(row == 20, top, jnp.where(row == 22, count - low(count), both))
    sz[...] = both.astype(BF16)
    rz[pl.ds(z, 1)] = sz[pl.ds(zlo, 1)]

    @pl.when(core == 1)
    def _():
        pl.semaphore_wait(barrier, 60)
        pl.semaphore_signal(far_sem, inc=1, device_id=sibling, device_id_type=MESH)

    @pl.when(core == 0)
    def _():
        pl.semaphore_wait(far_sem, 1)

    for z_to in z_peers:
        send(1, sz.at[lax.rem(z_to, 8)], rz.at[z], device(z_to, xy, core))
    wait(recv_sem.at[1], rz.at[pl.ds(0, ZN - 1)])
    slots, tops, totals = [], [], []
    for h in range(2):
        part = rz[pl.ds(8 * h, 8)].astype(F32)
        peaks = part[:, 20:21, :]
        top = jnp.max(peaks, axis=0)
        factor = jnp.exp(peaks - top)
        count = jnp.sum(factor * (part[:, 21:22, :] + part[:, 22:23, :]), axis=0)
        summed = jnp.sum(part * jnp.where(row < CH, factor, 1.0), axis=0)
        slots.append(jnp.where(row < CH, summed / count, summed))
        tops.append(top)
        totals.append(count)
        sb[pl.ds(2 * CH * h, 2 * CH), :] = slots[h][: 2 * CH]
    packed = sb[...].astype(BF16)
    rb[pl.ds(xy, 1)] = packed[None]

    for xy_to in xy_peers:
        send(2, rb.at[xy], rb.at[xy], device(z, xy_to, core))
    wait(recv_sem.at[2], rb.at[pl.ds(0, XYN - 1)])
    wide[...] = rb[...].astype(F32).reshape(XYN * PAIR, 128)

    def clips(first):
        return jnp.concatenate(
            [
                jnp.concatenate(
                    [wide[pl.ds(h * 2 * CH + first + j, 16, stride=PAIR), :].astype(BF16) for j in range(CH)],
                    axis=1,
                )
                for h in range(2)
            ],
            axis=0,
        )

    every_in, every_back = clips(0), clips(CH)
    pre = dot(every_in, w_in_v[0], ((1,), (1,)))
    act_back = dot(every_back, w_out_v[0], ((1,), (1,)))
    slope = math.sqrt(2.0 / math.pi)
    bent = jnp.tanh(slope * (pre + 0.044715 * (pre * pre * pre)))
    activated = (0.5 * pre * (1.0 + bent)).astype(BF16)
    gelu_slope = 0.5 * (1.0 + bent) + 0.5 * pre * ((1.0 + bent) * (1.0 - bent)) * (
        slope * (1.0 + 3.0 * 0.044715 * (pre * pre))
    )
    hidden_back = (gelu_slope * act_back).astype(BF16)
    in_part = dot(hidden_back, w_in_v[0], ((1,), (0,)))
    out_part = dot(activated, w_out_v[0], ((1,), (0,)))
    for h in range(2):
        for j in range(CH):
            wide[pl.ds(h * 2 * CH + j, 16, stride=PAIR), :] = chunk(in_part, j)[16 * h : 16 * h + 16]
            wide[pl.ds(h * 2 * CH + CH + j, 16, stride=PAIR), :] = chunk(out_part, j)[16 * h : 16 * h + 16]
    sc[...] = wide[...].reshape(XYN, PAIR, 128).astype(BF16)
    rc[pl.ds(xy, 1)] = sc[pl.ds(xy, 1)]

    for xy_to in xy_peers:
        send(3, sc.at[xy_to], rc.at[xy], device(z, xy_to, core))
    w_out_grad_v[0] = dot(activated, every_back, ((0,), (0,))).astype(BF16)
    w_in_grad_v[0] = dot(hidden_back, every_in, ((0,), (0,))).astype(BF16)
    wait(recv_sem.at[3], rc.at[pl.ds(0, XYN - 1)])
    halves[pl.ds(0, PAIR), :] = jnp.sum(rc[...].astype(F32), axis=0)
    for h in range(2):
        half = halves[pl.ds(2 * CH * h, REC), :]
        dotted = jnp.sum(jnp.where(row < CH, low(half) * slots[h], 0.0), keepdims=True)
        half = jnp.where(row == 20, tops[h], half)
        half = jnp.where(row == 21, totals[h], half)
        half = jnp.where(row == 22, totals[h] - low(totals[h]), half)
        half = jnp.where(row == 23, jnp.where(lane < 64, dotted, dotted - low(dotted)), half)
        sd[pl.ds(h, 1)] = half.astype(BF16)[None]
    rd[pl.ds(z, 1)] = sd[pl.ds(zhi, 1)]

    for z_to in z_peers:
        send(4, sd.at[z_to // 8], rd.at[z], device(z_to, xy, core))
    wait(recv_sem.at[4], rd.at[pl.ds(0, ZN - 1)])
    first, second = rd[pl.ds(0, 8)].astype(F32), rd[pl.ds(8, 8)].astype(F32)
    both = first + second
    dotted = both[:, 23:24, 0:1] + both[:, 23:24, 64:65]
    both = jnp.where(row == 20, first, both)
    both = jnp.where(row == 21, first[:, 21:22, :] + first[:, 22:23, :], both)
    both = jnp.where(row == 23, dotted, both)
    mine = pl.ds(pl.multiple_of(core * 192, 192), 192)
    se[mine, :] = both.reshape(192, 128)

    send(5, se.at[mine], se.at[mine], sibling)
    wait(recv_sem.at[5], ra)

    def slot_rows(first):
        return jnp.concatenate([se[pl.ds(first + j, 16, stride=REC), :] for j in range(CH)], axis=1).astype(BF16)

    in_back, slot_out = slot_rows(0), slot_rows(CH)
    col_peak = se[pl.ds(20, 16, stride=REC), :][:, 0:1]
    col_total = se[pl.ds(21, 16, stride=REC), :][:, 0:1]
    slot_total = se[pl.ds(23, 16, stride=REC), :][:, 0:1]
    dispatch = (jnp.exp(logits - col_peak) / col_total).astype(BF16)
    weights = dispatch.astype(F32)
    combine_back = dot(slot_out, grads_v[0], ((1,), (1,)))
    dispatch_back = dot(in_back, tokens_v[0], ((1,), (1,)))
    logit_comb = combine * (combine_back - jnp.sum(combine * combine_back, axis=0, keepdims=True))
    logit_back = (logit_comb + weights * (dispatch_back - slot_total)).astype(BF16)
    router_part = dot(logit_back, tokens_v[0], ((1,), (0,)))
    for j in range(CH):
        rows[pl.ds(j, 16, stride=16), :] = chunk(router_part, j)
    for j in range(CH, 16):
        rows[pl.ds(j, 16, stride=16), :] = jnp.zeros((16, 128), F32)
    sf[...] = rows[...].reshape(16, 16, 128).astype(BF16)
    rf[pl.ds(xy, 1)] = sf[pl.ds(xy, 1)]

    for xy_to in xy_peers:
        send(6, sf.at[xy_to], rf.at[xy], device(z, xy_to, core))
    left = jnp.concatenate([weights, logit_back.astype(F32)], axis=0).astype(BF16)
    right = jnp.concatenate([in_back.astype(F32), router], axis=0).astype(BF16)
    token_grad_v[0] = (dot(left, right, ((0,), (0,))) * 64.0).astype(BF16)
    wait(recv_sem.at[6], rf.at[pl.ds(0, XYN - 1)])
    own_row[...] = jnp.sum(rf[...].astype(F32), axis=0)
    send(9, own_row, other_row, sibling)
    wait(recv_sem.at[9], other_row)
    sh[...] = (own_row[...] + other_row[...]).astype(BF16)
    rh[pl.ds(z, 1)] = sh[...][None]

    for z_to in z_peers:
        send(7, sh, rh.at[z], device(z_to, xy, core))
    wait(recv_sem.at[7], rh.at[pl.ds(0, ZN - 1)])
    place = lax.rem(xy, 8) * 2 + xy // 8
    summed_row[...] = jnp.sum(rh[...].astype(F32), axis=0, keepdims=True).astype(BF16)

    for xy_to in xy_peers:
        send(8, summed_row.at[0], ri.at[place], device(z, xy_to, core))
    kept = pltpu.make_async_copy(summed_row.at[0], ri.at[place], out_sem.at[0])
    kept.start()
    wait(recv_sem.at[8], ri.at[pl.ds(0, 15)])

    wait(send_sem.at[0], ra)
    wait(send_sem.at[1], rz.at[pl.ds(0, ZN - 1)])
    wait(send_sem.at[2], rb.at[pl.ds(0, XYN - 1)])
    wait(send_sem.at[3], rc.at[pl.ds(0, XYN - 1)])
    wait(send_sem.at[4], rd.at[pl.ds(0, ZN - 1)])
    wait(send_sem.at[5], ra)
    wait(send_sem.at[6], rf.at[pl.ds(0, XYN - 1)])
    wait(send_sem.at[7], rh.at[pl.ds(0, ZN - 1)])
    wait(send_sem.at[8], ri.at[pl.ds(0, 15)])
    wait(send_sem.at[9], other_row)
    kept.wait()


def store_kernel(
    token_grad, ri, w_in_grad, w_out_grad,
    token_grad_hbm, router_grad_hbm, w_in_grad_hbm, w_out_grad_hbm,
    ri_v, rows, router_grad_v, sems,
):
    gather = pltpu.make_async_copy(ri, ri_v, sems.at[0])
    gather.start()
    copies = [
        pltpu.make_async_copy(token_grad, token_grad_hbm, sems.at[1]),
        pltpu.make_async_copy(w_in_grad, w_in_grad_hbm, sems.at[2]),
        pltpu.make_async_copy(w_out_grad, w_out_grad_hbm, sems.at[3]),
        pltpu.make_async_copy(router_grad_v, router_grad_hbm, sems.at[4]),
    ]
    for copy in copies[:3]:
        copy.start()
    gather.wait()
    rows[...] = (ri_v[...].astype(F32) / math.sqrt(32.0)).reshape(256, 128)
    for j in range(CH):
        router_grad_v[:, j * 128 : (j + 1) * 128] = rows[pl.ds(j, 16, stride=16), :]
    copies[3].start()
    for copy in copies:
        copy.wait()


def local(tokens, out_grad, logits, router, w_in, w_out):
    anywhere = pl.BlockSpec(memory_space=pl.ANY)
    vmem = pl.BlockSpec(memory_space=pltpu.VMEM)
    hbm = pl.BlockSpec(memory_space=pltpu.HBM)
    w_in = jnp.swapaxes(w_in, 1, 2)
    inputs = tuple(
        pltpu.with_memory_space_constraint(a, pltpu.HBM) for a in (tokens, out_grad, logits, router, w_in, w_out)
    )
    results = (
        jax.ShapeDtypeStruct(tokens.shape, BF16),
        jax.ShapeDtypeStruct(router.shape, F32),
        jax.ShapeDtypeStruct(w_in.shape, BF16),
        jax.ShapeDtypeStruct(w_out.shape, BF16),
    )
    made = pl.pallas_call(
        kernel,
        name="moe_back",
        out_shape=tuple(
            pltpu.VMEM(shape, BF16) for shape in (tokens.shape, (16, 16, 128), w_in.shape, w_out.shape)
        ),
        in_specs=[hbm] * 6,
        out_specs=(vmem, anywhere, vmem, vmem),
        scratch_shapes=[pltpu.VMEM(a.shape, a.dtype) for a in inputs]
        + [
            pltpu.VMEM((16 * REC, 128), F32),
            pltpu.VMEM((8 * REC, 128), F32),
            pltpu.VMEM((8, REC, 128), BF16),
            pltpu.VMEM((ZN, REC, 128), BF16),
            pltpu.VMEM((PAIR, 128), F32),
            pltpu.VMEM((XYN, PAIR, 128), BF16),
            pltpu.VMEM((XYN * PAIR, 128), F32),
            pltpu.VMEM((XYN, PAIR, 128), BF16),
            pltpu.VMEM((XYN, PAIR, 128), BF16),
            pltpu.VMEM((48, 128), F32),
            pltpu.VMEM((2, REC, 128), BF16),
            pltpu.VMEM((ZN, REC, 128), BF16),
            pltpu.VMEM((16 * REC, 128), F32),
            pltpu.VMEM((16 * 16, 128), F32),
            pltpu.VMEM((16, 16, 128), BF16),
            pltpu.VMEM((XYN, 16, 128), BF16),
            pltpu.VMEM((16, 128), F32),
            pltpu.VMEM((16, 128), F32),
            pltpu.VMEM((16, 128), BF16),
            pltpu.VMEM((ZN, 16, 128), BF16),
            pltpu.VMEM((1, 16, 128), BF16),
            pltpu.SemaphoreType.DMA((6,)),
            pltpu.SemaphoreType.DMA((4,)),
            pltpu.SemaphoreType.DMA((10,)),
            pltpu.SemaphoreType.DMA((10,)),
            pltpu.SemaphoreType.REGULAR,
            pltpu.SemaphoreType.REGULAR,
        ],
        compiler_params=pltpu.CompilerParams(
            collective_id=0, has_side_effects=True, vmem_limit_bytes=32 * 1024 * 1024
        ),
    )(*inputs)
    token_grad, router_grad, w_in_grad, w_out_grad = pl.pallas_call(
        store_kernel,
        name="store",
        out_shape=results,
        in_specs=[anywhere] * 4,
        out_specs=(hbm,) * 4,
        scratch_shapes=[
            pltpu.VMEM((16, 16, 128), BF16),
            pltpu.VMEM((256, 128), F32),
            pltpu.VMEM(router.shape, F32),
            pltpu.SemaphoreType.DMA((5,)),
        ],
    )(*(pltpu.with_memory_space_constraint(a, pltpu.VMEM) for a in made))
    return (token_grad, router_grad, jnp.swapaxes(w_in_grad, 1, 2), w_out_grad)


def solution(mesh):
    return jax.shard_map(
        local,
        mesh=mesh,
        in_specs=(
            P("dp", "seq", None),
            P("dp", "seq", None),
            P("dp", None, "seq"),
            P(),
            P("seq", None, "dp"),
            P("seq", "dp", None),
        ),
        out_specs=(P("dp", "seq", None), P(), P("seq", None, "dp"), P("seq", "dp", None)),
        check_vma=False,
    )
```
